32 devices in a mesh: pb: 8 (over z, y), ta: 2 (over x), row: 2 (over core).
Axes of the slice: x: 2, y: 2, z: 4, core: 2. Of those that a mesh axis runs over, the one named last changes fastest.
Arguments:
- query_features: bfloat16 [4096, 4096], P('pb', 'ta'), may hold values from -6 to 6
- inverse_gram: bfloat16 [4096, 4096], P('pb', 'ta'), may hold values from -0.03125 to 2.03125
- training_features: bfloat16 [2048, 4096], P(('row', 'ta'), 'pb'), parts along dimension 0, may hold values from -0.09375 to 0.09375
- residual_weight: float32 [2048], P(('row', 'ta')), parts along dimension 0, may hold values from 0.05 to 0.95
Outputs:
- scores: float32 [4096, 2048], P('pb', ('row', 'ta')), parts along dimension 1
The draws below stay inside these ranges and needn't reach their ends.
There are 2 independent parts, one for each index of `row`. The reference program is written for one: setup_inputs(seed, part) draws one part's arguments, and reference() takes and returns one part's arrays. A program takes and returns all parts, laid end to end along the dimension named above; an argument that names none is the same for every part. Nothing has to cross between parts.
All inputs are finite; a program needn't handle non-finite values.
Results may differ from the reference program's by a relative error of at most 0.0029.
Values may be sent and summed in bfloat16 or wider, within the bound.
A program may use at most 64 MiB of HBM per device.

```python
import jax
import jax.numpy as jnp
from jax import lax

P_SIZE = 4096
NQ = 4096
NT = 1024


def draw_inverse_gram(key, part):
    key = jax.random.fold_in(key, 5)
    noise_key, diag_key = jax.random.split(key)
    spread = 0.5 / P_SIZE ** 0.5
    noise = jnp.clip(jax.random.normal(noise_key, (P_SIZE, P_SIZE), jnp.float32), -3.5, 3.5) * spread
    diagonal = jnp.exp(jax.random.uniform(diag_key, (P_SIZE,), jnp.float32, -0.69, 0.69))
    rows_idx = lax.broadcasted_iota(jnp.int32, (P_SIZE, P_SIZE), 0)
    cols_idx = lax.broadcasted_iota(jnp.int32, (P_SIZE, P_SIZE), 1)
    identity = (rows_idx == cols_idx).astype(jnp.float32)
    return (noise + identity * diagonal[:, None]).astype(jnp.bfloat16)


def level_of(stream_key, dims, cuts, smallest, high):
    def one(position, shards_of):
        heights = jax.random.uniform(jax.random.fold_in(jax.random.fold_in(stream_key, 6), position), (shards_of,), jnp.float32, smallest / len(cuts), high / len(cuts))
        return jnp.repeat(jnp.exp(heights), dims[position] // shards_of).reshape((-1,) + (1,) * (len(dims) - position - 1))

    loudness = one(*cuts[0])
    for cut in cuts[1:]:
        loudness = loudness * one(*cut)
    return loudness


def scatter_about(stream_key, extent, width, reach, cuts=(), kind=jnp.bfloat16):
    drawn = jax.random.normal(stream_key, extent, jnp.float32) * width
    if len(cuts) > 0:
        drawn = level_of(stream_key, extent, cuts, -0.22, 0.18) * drawn
    return jnp.clip(drawn, min=-reach, max=reach).astype(kind)


def setup_inputs(seed: int = 0, part: int = 0) -> dict:
    key_of = jax.random.split(jax.random.key(seed), 5)
    part_splits = jax.random.split(jax.random.fold_in(key_of[4], part), 5)
    return {
        "query_features": scatter_about(key_of[0], (NQ, P_SIZE), 1.0, 6.0, ((0, 8), (1, 2))),
        "inverse_gram": draw_inverse_gram(jax.random.fold_in(key_of[4], 71), part),
        "training_features": scatter_about(part_splits[2], (NT, P_SIZE), P_SIZE ** -0.5, 0.09375, ((0, 2), (1, 8))),
        "residual_weight": jnp.clip(0.05 + 0.9 * jax.random.uniform(part_splits[3], (NT,), jnp.float32) ** level_of(part_splits[3], (NT,), ((0, 2),), -0.2, 0.2), 0.05, 0.95),
    }


def reference(query_features, inverse_gram, training_features, residual_weight):
    preconditioned = jnp.dot(query_features, inverse_gram, preferred_element_type=jnp.float32).astype(jnp.bfloat16)
    raw = jnp.dot(preconditioned, training_features.T, preferred_element_type=jnp.float32)
    return raw * residual_weight[None, :]
```

```python
import functools

import jax
import jax.numpy as jnp
from jax import lax
from jax.experimental import pallas as pl
from jax.experimental.pallas import tpu as pltpu
from jax.sharding import PartitionSpec as P

MESH = pl.DeviceIdType.MESH
PARTS = 4


def kernel(npb, nc, q_ref, g_ref, t_ref, out_ref, q_all, g_all, t_all, h_all,
           own_sem, send_sem, recv_sem, x_send, x_recv, s_send, s_recv):
    me = lax.axis_index("pb")
    ta = lax.axis_index("ta")
    row = lax.axis_index("row")
    nz = npb // 2
    z, y = me // 2, me % 2
    up, down, across = {"pb": me + 2}, {"pb": me - 2}, {"pb": z * 2 + 1 - y}
    xp, sib = {"ta": 1 - ta}, {"row": 1 - row}
    rows, half = g_ref.shape
    ex, feats = t_ref.shape
    width = ex // nc
    lag = nc // 2
    has_up, has_down = z < nz - 1, z > 0

    mine = pl.ds(pl.multiple_of(ta * half, half), half)
    own_t = pltpu.make_async_copy(t_ref, t_all.at[:, pl.ds(pl.multiple_of(me * feats, feats), feats)], own_sem.at[0])
    own_g = pltpu.make_async_copy(g_ref, g_all.at[:, mine], own_sem.at[1])
    own_q = pltpu.make_async_copy(q_ref, q_all.at[:, mine], own_sem.at[2])
    own_t.start()
    own_g.start()
    own_q.start()

    barrier = pltpu.get_barrier_semaphore()

    def greet(device):
        pl.semaphore_signal(barrier, inc=1, device_id=device, device_id_type=MESH)

    for device in (across, xp, sib):
        greet(device)
    pl.when(has_up)(lambda: greet(up))
    pl.when(has_down)(lambda: greet(down))
    pl.semaphore_wait(barrier, 3 + has_up.astype(jnp.int32) + has_down.astype(jnp.int32))

    def place(phase, c, b):
        if phase == 0:
            return t_all.at[pl.ds(pl.multiple_of(c * width, width), width), pl.ds(pl.multiple_of(b * feats, feats), feats)]
        return h_all.at[c, pl.ds(pl.multiple_of(b * rows, rows), rows)]

    def copy(phase, c, b, way, device):
        ref = place(phase, c, b)
        return pltpu.make_async_remote_copy(
            src_ref=ref, dst_ref=ref, send_sem=send_sem.at[phase, c, way, b], recv_sem=recv_sem.at[phase, c, b],
            device_id=device, device_id_type=MESH)

    def send_own(phase, c):
        pl.when(has_up)(lambda: copy(phase, c, me, 0, up).start())
        pl.when(has_down)(lambda: copy(phase, c, me, 1, down).start())
        copy(phase, c, me, 2, across).start()

    def arrivals(phase, c):
        for d in range(1, nz):
            @pl.when(z - d >= 0)
            def _():
                b = me - 2 * d
                copy(phase, c, b, 0, across).wait_recv()
                pl.when(has_up)(lambda: copy(phase, c, b, 0, up).start())
                copy(phase, c, b, 2, across).start()

            @pl.when(z + d < nz)
            def _():
                b = me + 2 * d
                copy(phase, c, b, 0, across).wait_recv()
                pl.when(has_down)(lambda: copy(phase, c, b, 1, down).start())
                copy(phase, c, b, 2, across).start()

    def arrivals_across(phase, c):
        for other in range(nz):
            copy(phase, c, other * 2 + 1 - y, 2, across).wait_recv()

    def finish_sends(phase, c):
        for other in range(nz):
            b = other * 2 + y
            pl.when(has_up & (other <= z))(lambda: copy(phase, c, b, 0, up).wait_send())
            pl.when(has_down & (other >= z))(lambda: copy(phase, c, b, 1, down).wait_send())
            copy(phase, c, b, 2, across).wait_send()

    piece = rows // 2 // PARTS

    def strip(which, i, r, t):
        whole = (g_all, q_all)[which]
        return whole.at[pl.ds(pl.multiple_of(r * (rows // 2) + i * piece, piece), piece), pl.ds(pl.multiple_of(t * half, half), half)]

    def x_copy(which, i, t):
        ref = strip(which, i, row, t)
        return pltpu.make_async_remote_copy(
            src_ref=ref, dst_ref=ref, send_sem=x_send.at[which, i], recv_sem=x_recv.at[which, i],
            device_id=xp, device_id_type=MESH)

    def s_copy(which, i, r):
        ref = strip(which, i, r, 1 - ta)
        return pltpu.make_async_remote_copy(
            src_ref=ref, dst_ref=ref, send_sem=s_send.at[which, i], recv_sem=s_recv.at[which, i],
            device_id=sib, device_id_type=MESH)

    def pass_on(which, pieces):
        for i in pieces:
            x_copy(which, i, 1 - ta).wait_recv()
            s_copy(which, i, row).start()

    def from_sibling(which):
        for i in range(PARTS):
            s_copy(which, i, 1 - row).wait_recv()

    own_t.wait()
    send_own(0, 0)
    own_g.wait()
    for i in range(PARTS):
        x_copy(0, i, ta).start()
    own_q.wait()

    def step(s, carry):
        pl.when(s + 1 < nc)(lambda: send_own(0, s + 1))
        pl.when(s < nc)(lambda: arrivals(0, s))

        @pl.when(s == 0)
        def _():
            pass_on(0, range(PARTS // 2))

        @pl.when(s == lag - 1)
        def _():
            pass_on(0, range(PARTS // 2, PARTS))
            for i in range(PARTS):
                x_copy(1, i, ta).start()
            from_sibling(0)

        @pl.when((s >= lag) & (s < nc + lag))
        def _():
            c = s - lag
            arrivals_across(0, c)
            span = pl.ds(pl.multiple_of(c * width, width), width)
            h = lax.dot_general(g_all[...], t_all[span, :], (((1,), (1,)), ((), ())), preferred_element_type=jnp.float32)
            h_all[c, pl.ds(pl.multiple_of(me * rows, rows), rows), :] = h.astype(jnp.bfloat16)
            send_own(1, c)

        @pl.when(s == nc - 1)
        def _():
            pass_on(1, range(PARTS // 2))

        @pl.when(s >= nc)
        def _():
            c = s - nc
            arrivals(1, c)

            @pl.when(s == nc)
            def _():
                pass_on(1, range(PARTS // 2, PARTS))
                from_sibling(1)

            arrivals_across(1, c)
            span = pl.ds(pl.multiple_of(c * width, width), width)
            out_ref[:, span] = jnp.dot(q_all[...], h_all[c], preferred_element_type=jnp.float32)

        return carry

    lax.fori_loop(0, 2 * nc, step, 0)

    def drain(c, carry):
        finish_sends(0, c)
        finish_sends(1, c)
        return carry

    lax.fori_loop(0, nc, drain, 0)
    for which in range(2):
        for i in range(PARTS):
            x_copy(which, i, ta).wait_send()
            s_copy(which, i, row).wait_send()


def by_kernel(npb, query, gram, training, weight):
    rows, half = gram.shape
    ex, feats = training.shape
    queries = query.shape[0]
    nc = ex // 128
    width = ex // nc
    anywhere = pl.BlockSpec(memory_space=pl.ANY)
    raw = pl.pallas_call(
        functools.partial(kernel, npb, nc),
        out_shape=jax.ShapeDtypeStruct((queries, ex), jnp.float32),
        in_specs=[anywhere] * 3,
        out_specs=pl.BlockSpec(memory_space=pltpu.VMEM),
        scratch_shapes=[
            pltpu.VMEM((queries, 2 * half), jnp.bfloat16),
            pltpu.VMEM((rows, 2 * half), jnp.bfloat16),
            pltpu.VMEM((ex, npb * feats), jnp.bfloat16),
            pltpu.VMEM((nc, npb * rows, width), jnp.bfloat16),
            pltpu.SemaphoreType.DMA((3,)),
            pltpu.SemaphoreType.DMA((2, nc, 3, npb)),
            pltpu.SemaphoreType.DMA((2, nc, npb)),
            pltpu.SemaphoreType.DMA((2, PARTS)),
            pltpu.SemaphoreType.DMA((2, PARTS)),
            pltpu.SemaphoreType.DMA((2, PARTS)),
            pltpu.SemaphoreType.DMA((2, PARTS)),
        ],
        compiler_params=pltpu.CompilerParams(collective_id=0, has_side_effects=True, vmem_limit_bytes=48 * 2**20),
        cost_estimate=pl.CostEstimate(
            flops=2 * (rows + queries) * ex * 2 * half, bytes_accessed=2 * (2 * rows * half + ex * feats) + 4 * queries * ex,
            transcendentals=0),
    )(query, gram, training)
    return raw * weight[None, :]


def by_gathers(query, gram, training, weight):
    whole_gram = lax.all_gather(gram, "ta", axis=1, tiled=True)
    whole_training = lax.all_gather(training, "pb", axis=1, tiled=True)
    mapped = lax.dot_general(
        whole_gram, whole_training, (((1,), (1,)), ((), ())), preferred_element_type=jnp.float32).astype(jnp.bfloat16)
    whole_query = lax.all_gather(query, "ta", axis=1, tiled=True)
    whole_mapped = lax.all_gather(mapped, "pb", axis=0, tiled=True)
    return jnp.dot(whole_query, whole_mapped, preferred_element_type=jnp.float32) * weight[None, :]


def solution(mesh):
    npb, nta, nrow = mesh.shape["pb"], mesh.shape["ta"], mesh.shape["row"]

    def local(query, gram, training, weight):
        fits = nta == 2 and nrow == 2 and npb % 2 == 0 and query.shape == gram.shape and training.shape[0] % 256 == 0
        if fits:
            return by_kernel(npb, query, gram, training, weight)
        return by_gathers(query, gram, training, weight)

    placed = (P("pb", "ta"), P("pb", "ta"), P(("row", "ta"), "pb"), P(("row", "ta")))
    return jax.shard_map(
        local, mesh=mesh, in_specs=placed, out_specs=P("pb", ("row", "ta")), check_vma=False
    )
```

```python
import functools

import jax
import jax.numpy as jnp
from jax import lax
from jax.experimental import pallas as pl
from jax.experimental.pallas import tpu as pltpu
from jax.sharding import PartitionSpec as P

MESH = pl.DeviceIdType.MESH
SUB = 2


def kernel(npb, nc, q_ref, g_ref, t_ref, out_ref, q_all, g_all, t_all, h_all, kept, part_out, part_in,
           own_sem, z_send, z_recv, y_send, y_recv, x_send, x_recv, s_send, s_recv, p_send, p_recv):
    me = lax.axis_index("pb")
    ta = lax.axis_index("ta")
    row = lax.axis_index("row")
    nz = npb // 2
    z, y = me // 2, me % 2
    up, down, across = {"pb": me + 2}, {"pb": me - 2}, {"pb": z * 2 + 1 - y}
    xp, sib = {"ta": 1 - ta}, {"row": 1 - row}
    rows, half = g_ref.shape
    ex, feats = t_ref.shape
    width = ex // nc
    nh = half // feats // 2
    strip_rows = rows // 2
    has_up, has_down = z < nz - 1, z > 0

    def remote(src, dst, send_sem, recv_sem, device):
        return pltpu.make_async_remote_copy(
            src_ref=src, dst_ref=dst, send_sem=send_sem, recv_sem=recv_sem, device_id=device, device_id_type=MESH)

    def at(start, size):
        return pl.ds(pl.multiple_of(start * size, size), size)

    def own_columns(which, j, which_y, rows_at):
        return (g_ref, q_ref)[which].at[rows_at, at(j * 2 + which_y, feats)]

    def strip(which, which_y, r, block):
        return (g_all, q_all)[which].at[at(which_y * 2 + r, strip_rows), at(block, feats)]

    own_t = pltpu.make_async_copy(t_ref, t_all.at[:, at(z, feats)], own_sem.at[0])
    own_t.start()
    own = [
        pltpu.make_async_copy(
            own_columns(which, j, y, pl.ds(0, rows)),
            (g_all, q_all)[which].at[at(y, rows), at(ta * nh + j, feats)], own_sem.at[1 + which * nh + j])
        for which in range(2) for j in range(nh)
    ]

    barrier = pltpu.get_barrier_semaphore()

    def greet(device):
        pl.semaphore_signal(barrier, inc=1, device_id=device, device_id_type=MESH)

    for device in (across, xp, sib):
        greet(device)
    pl.when(has_up)(lambda: greet(up))
    pl.when(has_down)(lambda: greet(down))
    pl.semaphore_wait(barrier, 3 + has_up.astype(jnp.int32) + has_down.astype(jnp.int32))

    def place(phase, c, i, block):
        if phase == 0:
            return t_all.at[at(c * SUB + i, width // SUB), at(block, feats)]
        return h_all.at[c, at(block * SUB + i, rows // SUB)]

    def z_copy(phase, c, i, block, way):
        ref = place(phase, c, i, block)
        return remote(ref, ref, z_send.at[phase, c, i, way, block], z_recv.at[phase, c, i, block], (up, down)[way])

    def send_own(phase, c):
        for i in range(SUB):
            pl.when(has_up)(lambda: z_copy(phase, c, i, z, 0).start())
            pl.when(has_down)(lambda: z_copy(phase, c, i, z, 1).start())

    def arrivals(phase, c):
        for d in range(1, nz):
            for i in range(SUB):
                @pl.when(z - d >= 0)
                def _():
                    z_copy(phase, c, i, z - d, 0).wait_recv()
                    pl.when(has_up)(lambda: z_copy(phase, c, i, z - d, 0).start())

                @pl.when(z + d < nz)
                def _():
                    z_copy(phase, c, i, z + d, 1).wait_recv()
                    pl.when(has_down)(lambda: z_copy(phase, c, i, z + d, 1).start())

    def finish_sends(phase, c):
        for i in range(SUB):
            for block in range(nz):
                pl.when(has_up & (block <= z))(lambda: z_copy(phase, c, i, block, 0).wait_send())
                pl.when(has_down & (block >= z))(lambda: z_copy(phase, c, i, block, 1).wait_send())

    def y_out(which, j):
        return remote(
            own_columns(which, j, 1 - y, at(row, strip_rows)), strip(which, y, row, ta * nh + j),
            y_send.at[which, j], y_recv.at[which, j], across)

    def y_in(which, j):
        ref = strip(which, 1 - y, row, ta * nh + j)
        return remote(ref, ref, y_send.at[which, j], y_recv.at[which, j], across)

    def x_out(which, kind, j):
        dst = strip(which, (y, 1 - y)[kind], row, ta * nh + j)
        src = own_columns(which, j, y, at(row, strip_rows)) if kind == 0 else dst
        return remote(src, dst, x_send.at[which, kind, j], x_recv.at[which, kind, j], xp)

    def x_in(which, kind, j):
        ref = strip(which, (y, 1 - y)[kind], row, (1 - ta) * nh + j)
        return remote(ref, ref, x_send.at[which, kind, j], x_recv.at[which, kind, j], xp)

    def s_copy(which, kind, j, r):
        ref = strip(which, (y, 1 - y, 1 - y)[kind], r, (ta if kind == 2 else 1 - ta) * nh + j)
        return remote(ref, ref, s_send.at[which, kind, j], s_recv.at[which, kind, j], sib)

    def from_y(which):
        for j in range(nh):
            y_in(which, j).wait_recv()
            x_out(which, 1, j).start()
            s_copy(which, 2, j, row).start()

    def from_x(which, kind):
        for j in range(nh):
            x_in(which, kind, j).wait_recv()
            s_copy(which, kind, j, row).start()

    def from_sibling(which):
        for kind in range(3):
            for j in range(nh):
                s_copy(which, kind, j, 1 - row).wait_recv()

    def p_copy(phase, c):
        return remote(part_out.at[phase, c], part_in.at[phase, c], p_send.at[phase, c], p_recv.at[phase, c], across)

    def h_partial(c, carry):
        examples = t_all[at(c, width), :]

        def product(which_y):
            return lax.dot_general(
                g_all[at(which_y, rows), :], examples, (((1,), (1,)), ((), ())), preferred_element_type=jnp.float32)

        part_out[0, c] = product(1 - y)
        p_copy(0, c).start()
        kept[c] = product(y)
        return carry

    def h_combine(c):
        p_copy(0, c).wait_recv()
        h_all[c, at(z, rows), :] = (kept[c] + part_in[0, c]).astype(jnp.bfloat16)
        send_own(1, c)

    def score_partial(c):
        def product(which_y):
            return jnp.dot(q_all[at(which_y, rows), :], h_all[c], preferred_element_type=jnp.float32)

        part_out[1, c] = product(1 - y)
        p_copy(1, c).start()
        out_ref[:, at(c, width)] = product(y)

    def score_combine(c):
        p_copy(1, c).wait_recv()
        out_ref[:, at(c, width)] += part_in[1, c]

    own_t.wait()
    send_own(0, 0)
    for j in range(nh):
        y_out(0, j).start()
        x_out(0, 0, j).start()
    for copy in own:
        copy.start()
    for j in range(nh):
        y_out(1, j).start()

    def step(s, carry):
        pl.when(s + 1 < nc)(lambda: send_own(0, s + 1))
        pl.when(s < nc)(lambda: arrivals(0, s))

        @pl.when(s == 0)
        def _():
            from_y(0)

        @pl.when(s == 1)
        def _():
            from_x(0, 0)

        @pl.when(s == 2)
        def _():
            from_x(0, 1)
            for j in range(nh):
                x_out(1, 0, j).start()
            from_y(1)
            for copy in own:
                copy.wait()
            from_sibling(0)

        lax.fori_loop(jnp.where(s <= 2, 0, s - 1), jnp.where(s < 2, 0, jnp.minimum(s, nc)), h_partial, 0)
        pl.when((s >= 3) & (s < nc + 3))(lambda: h_combine(s - 3))

        @pl.when(s == nc - 1)
        def _():
            from_x(1, 0)

        @pl.when(s >= nc)
        def _():
            c = s - nc
            arrivals(1, c)

            @pl.when(s == nc)
            def _():
                from_x(1, 1)
                from_sibling(1)

            score_partial(c)
            pl.when(c >= 2)(lambda: score_combine(c - 2))

        return carry

    lax.fori_loop(0, 2 * nc, step, 0)
    score_combine(nc - 2)
    score_combine(nc - 1)

    def drain(c, carry):
        for phase in range(2):
            finish_sends(phase, c)
            p_copy(phase, c).wait_send()
        return carry

    lax.fori_loop(0, nc, drain, 0)
    for which in range(2):
        for j in range(nh):
            y_out(which, j).wait_send()
            for kind in range(2):
                x_out(which, kind, j).wait_send()
            for kind in range(3):
                s_copy(which, kind, j, row).wait_send()


def by_kernel(npb, query, gram, training, weight):
    rows, half = gram.shape
    ex, feats = training.shape
    width = 128
    nc = ex // width
    nz = npb // 2
    nh = half // feats // 2
    anywhere = pl.BlockSpec(memory_space=pl.ANY)
    dma = pltpu.SemaphoreType.DMA
    raw = pl.pallas_call(
        functools.partial(kernel, npb, nc),
        out_shape=jax.ShapeDtypeStruct((rows, ex), jnp.float32),
        in_specs=[anywhere] * 3,
        out_specs=pl.BlockSpec(memory_space=pltpu.VMEM),
        scratch_shapes=[
            pltpu.VMEM((2 * rows, half), jnp.bfloat16),
            pltpu.VMEM((2 * rows, half), jnp.bfloat16),
            pltpu.VMEM((ex, half), jnp.bfloat16),
            pltpu.VMEM((nc, half, width), jnp.bfloat16),
            pltpu.VMEM((nc, rows, width), jnp.float32),
            pltpu.VMEM((2, nc, rows, width), jnp.float32),
            pltpu.VMEM((2, nc, rows, width), jnp.float32),
            dma((1 + 2 * nh,)),
            dma((2, nc, SUB, 2, nz)),
            dma((2, nc, SUB, nz)),
            dma((2, nh)),
            dma((2, nh)),
            dma((2, 2, nh)),
            dma((2, 2, nh)),
            dma((2, 3, nh)),
            dma((2, 3, nh)),
            dma((2, nc)),
            dma((2, nc)),
        ],
        compiler_params=pltpu.CompilerParams(collective_id=0, has_side_effects=True, vmem_limit_bytes=60 * 2**20),
        cost_estimate=pl.CostEstimate(
            flops=8 * rows * ex * half, bytes_accessed=2 * (2 * rows * half + ex * feats) + 4 * rows * ex, transcendentals=0),
    )(query, gram, training)
    return raw * weight[None, :]


def by_gathers(query, gram, training, weight):
    whole_gram = lax.all_gather(gram, "ta", axis=1, tiled=True)
    whole_training = lax.all_gather(training, "pb", axis=1, tiled=True)
    mapped = lax.dot_general(
        whole_gram, whole_training, (((1,), (1,)), ((), ())), preferred_element_type=jnp.float32).astype(jnp.bfloat16)
    whole_query = lax.all_gather(query, "ta", axis=1, tiled=True)
    whole_mapped = lax.all_gather(mapped, "pb", axis=0, tiled=True)
    return jnp.dot(whole_query, whole_mapped, preferred_element_type=jnp.float32) * weight[None, :]


def solution(mesh):
    npb, nta, nrow = mesh.shape["pb"], mesh.shape["ta"], mesh.shape["row"]

    def local(query, gram, training, weight):
        ex, feats = training.shape
        square = query.shape == gram.shape == (feats, npb // 2 * feats)
        fits = (
            nta == 2 and nrow == 2 and npb % 4 == 0 and square
            and ex % 128 == 0 and ex >= 384 and feats % 128 == 0)
        if fits:
            return by_kernel(npb, query, gram, training, weight)
        return by_gathers(query, gram, training, weight)

    placed = (P("pb", "ta"), P("pb", "ta"), P(("row", "ta"), "pb"), P(("row", "ta")))
    return jax.shard_map(
        local, mesh=mesh, in_specs=placed, out_specs=P("pb", ("row", "ta")), check_vma=False
    )
```

```python
import functools

import jax
import jax.numpy as jnp
from jax import lax
from jax.experimental import pallas as pl
from jax.experimental.pallas import tpu as pltpu
from jax.sharding import PartitionSpec as P

MESH = pl.DeviceIdType.MESH
SUB = 2


def kernel(npb, nc, q_ref, g_ref, t_ref, out_ref, q_all, g_all, t_all, h_all, kept, part_out, part_in,
           own_sem, z_send, z_recv, y_send, y_recv, x_send, x_recv, s_send, s_recv, p_send, p_recv):
    me = lax.axis_index("pb")
    ta = lax.axis_index("ta")
    row = lax.axis_index("row")
    nz = npb // 2
    z, y = me // 2, me % 2
    up, down, across = {"pb": me + 2}, {"pb": me - 2}, {"pb": z * 2 + 1 - y}
    xp, sib = {"ta": 1 - ta}, {"row": 1 - row}
    rows, half = g_ref.shape
    ex, feats = t_ref.shape
    width = ex // nc
    nh = half // feats // 2
    strip_rows = rows // 2
    has_up, has_down = z < nz - 1, z > 0

    def remote(src, dst, send_sem, recv_sem, device):
        return pltpu.make_async_remote_copy(
            src_ref=src, dst_ref=dst, send_sem=send_sem, recv_sem=recv_sem, device_id=device, device_id_type=MESH)

    def at(start, size):
        return pl.ds(pl.multiple_of(start * size, size), size)

    def own_columns(which, j, which_y, rows_at):
        return (g_ref, q_ref)[which].at[rows_at, at(j * 2 + which_y, feats)]

    def strip(which, which_y, r, block):
        return (g_all, q_all)[which].at[at(which_y * 2 + r, strip_rows), at(block, feats)]

    own_t = pltpu.make_async_copy(t_ref, t_all.at[:, at(z, feats)], own_sem.at[0])
    own_t.start()
    own = [
        pltpu.make_async_copy(
            own_columns(which, j, y, pl.ds(0, rows)),
            (g_all, q_all)[which].at[at(y, rows), at(ta * nh + j, feats)], own_sem.at[1 + which * nh + j])
        for which in range(2) for j in range(nh)
    ]

    barrier = pltpu.get_barrier_semaphore()

    def greet(device):
        pl.semaphore_signal(barrier, inc=1, device_id=device, device_id_type=MESH)

    for device in (across, xp, sib):
        greet(device)
    pl.when(has_up)(lambda: greet(up))
    pl.when(has_down)(lambda: greet(down))
    pl.semaphore_wait(barrier, 3 + has_up.astype(jnp.int32) + has_down.astype(jnp.int32))

    def place(phase, c, i, block):
        if phase == 0:
            return t_all.at[at(c * SUB + i, width // SUB), at(block, feats)]
        return h_all.at[c, at(block * SUB + i, rows // SUB)]

    def z_copy(phase, c, i, block, way):
        ref = place(phase, c, i, block)
        return remote(ref, ref, z_send.at[phase, c, i, way, block], z_recv.at[phase, c, i, block], (up, down)[way])

    def send_own(phase, c):
        for i in range(SUB):
            pl.when(has_up)(lambda: z_copy(phase, c, i, z, 0).start())
            pl.when(has_down)(lambda: z_copy(phase, c, i, z, 1).start())

    def arrivals(phase, c):
        for d in range(1, nz):
            for i in range(SUB):
                @pl.when(z - d >= 0)
                def _():
                    z_copy(phase, c, i, z - d, 0).wait_recv()
                    pl.when(has_up)(lambda: z_copy(phase, c, i, z - d, 0).start())

                @pl.when(z + d < nz)
                def _():
                    z_copy(phase, c, i, z + d, 1).wait_recv()
                    pl.when(has_down)(lambda: z_copy(phase, c, i, z + d, 1).start())

    def finish_sends(phase, c):
        for i in range(SUB):
            for block in range(nz):
                pl.when(has_up & (block <= z))(lambda: z_copy(phase, c, i, block, 0).wait_send())
                pl.when(has_down & (block >= z))(lambda: z_copy(phase, c, i, block, 1).wait_send())

    def y_out(which, j):
        return remote(
            own_columns(which, j, 1 - y, at(row, strip_rows)), strip(which, y, row, ta * nh + j),
            y_send.at[which, j], y_recv.at[which, j], across)

    def y_in(which, j):
        ref = strip(which, 1 - y, row, ta * nh + j)
        return remote(ref, ref, y_send.at[which, j], y_recv.at[which, j], across)

    def x_out(which, kind, j):
        dst = strip(which, (y, 1 - y)[kind], row, ta * nh + j)
        src = own_columns(which, j, y, at(row, strip_rows)) if kind == 0 else dst
        return remote(src, dst, x_send.at[which, kind, j], x_recv.at[which, kind, j], xp)

    def x_in(which, kind, j):
        ref = strip(which, (y, 1 - y)[kind], row, (1 - ta) * nh + j)
        return remote(ref, ref, x_send.at[which, kind, j], x_recv.at[which, kind, j], xp)

    def s_copy(which, kind, j, r):
        ref = strip(which, (y, 1 - y, 1 - y)[kind], r, (ta if kind == 2 else 1 - ta) * nh + j)
        return remote(ref, ref, s_send.at[which, kind, j], s_recv.at[which, kind, j], sib)

    def from_y(which):
        for j in range(nh):
            y_in(which, j).wait_recv()
            x_out(which, 1, j).start()
            s_copy(which, 2, j, row).start()

    def from_x(which, kind):
        for j in range(nh):
            x_in(which, kind, j).wait_recv()
            s_copy(which, kind, j, row).start()

    def from_sibling(which):
        for kind in range(3):
            for j in range(nh):
                s_copy(which, kind, j, 1 - row).wait_recv()

    def p_copy(phase, c):
        return remote(part_out.at[phase, c], part_in.at[phase, c], p_send.at[phase, c], p_recv.at[phase, c], across)

    def h_partial(c, carry):
        examples = t_all[at(c, width), :]

        def product(which_y):
            return lax.dot_general(
                g_all[at(which_y, rows), :], examples, (((1,), (1,)), ((), ())), preferred_element_type=jnp.float32)

        part_out[0, c] = product(1 - y)
        p_copy(0, c).start()
        kept[c] = product(y)
        return carry

    def h_combine(c):
        p_copy(0, c).wait_recv()
        h_all[c, at(z, rows), :] = (kept[c] + part_in[0, c]).astype(jnp.bfloat16)
        send_own(1, c)

    def score_partial(c):
        def product(which_y):
            return jnp.dot(q_all[at(which_y, rows), :], h_all[c], preferred_element_type=jnp.float32)

        part_out[1, c] = product(1 - y)
        p_copy(1, c).start()
        out_ref[:, at(c, width)] = product(y)

    def score_combine(c):
        p_copy(1, c).wait_recv()
        out_ref[:, at(c, width)] += part_in[1, c]

    own_t.wait()
    send_own(0, 0)
    for j in range(nh):
        y_out(0, j).start()
        x_out(0, 0, j).start()
    for copy in own:
        copy.start()

    def step(s, carry):
        pl.when(s + 1 < nc)(lambda: send_own(0, s + 1))
        pl.when(s < nc)(lambda: arrivals(0, s))

        @pl.when(s == 0)
        def _():
            from_y(0)
            for j in range(nh):
                y_out(1, j).start()

        @pl.when(s == 1)
        def _():
            from_x(0, 0)

        @pl.when(s == 2)
        def _():
            from_x(0, 1)
            for j in range(nh):
                x_out(1, 0, j).start()
            from_y(1)
            for copy in own:
                copy.wait()
            from_sibling(0)

        lax.fori_loop(jnp.where(s <= 2, 0, s - 1), jnp.where(s < 2, 0, jnp.minimum(s, nc)), h_partial, 0)
        pl.when((s >= 3) & (s < nc + 3))(lambda: h_combine(s - 3))

        @pl.when(s == nc - 1)
        def _():
            from_x(1, 0)

        @pl.when(s >= nc)
        def _():
            c = s - nc

            @pl.when(c == 1)
            def _():
                from_x(1, 1)
                from_sibling(1)

            pl.when(c >= 1)(lambda: score_partial(c - 1))
            arrivals(1, c)
            pl.when(c >= 2)(lambda: score_combine(c - 2))

        return carry

    lax.fori_loop(0, 2 * nc, step, 0)
    score_partial(nc - 1)
    score_combine(nc - 2)
    score_combine(nc - 1)

    def drain(c, carry):
        for phase in range(2):
            finish_sends(phase, c)
            p_copy(phase, c).wait_send()
        return carry

    lax.fori_loop(0, nc, drain, 0)
    for which in range(2):
        for j in range(nh):
            y_out(which, j).wait_send()
            for kind in range(2):
                x_out(which, kind, j).wait_send()
            for kind in range(3):
                s_copy(which, kind, j, row).wait_send()


def by_kernel(npb, query, gram, training, weight):
    rows, half = gram.shape
    ex, feats = training.shape
    width = 128
    nc = ex // width
    nz = npb // 2
    nh = half // feats // 2
    anywhere = pl.BlockSpec(memory_space=pl.ANY)
    dma = pltpu.SemaphoreType.DMA
    raw = pl.pallas_call(
        functools.partial(kernel, npb, nc),
        out_shape=jax.ShapeDtypeStruct((rows, ex), jnp.float32),
        in_specs=[anywhere] * 3,
        out_specs=pl.BlockSpec(memory_space=pltpu.VMEM),
        scratch_shapes=[
            pltpu.VMEM((2 * rows, half), jnp.bfloat16),
            pltpu.VMEM((2 * rows, half), jnp.bfloat16),
            pltpu.VMEM((ex, half), jnp.bfloat16),
            pltpu.VMEM((nc, half, width), jnp.bfloat16),
            pltpu.VMEM((nc, rows, width), jnp.float32),
            pltpu.VMEM((2, nc, rows, width), jnp.float32),
            pltpu.VMEM((2, nc, rows, width), jnp.float32),
            dma((1 + 2 * nh,)),
            dma((2, nc, SUB, 2, nz)),
            dma((2, nc, SUB, nz)),
            dma((2, nh)),
            dma((2, nh)),
            dma((2, 2, nh)),
            dma((2, 2, nh)),
            dma((2, 3, nh)),
            dma((2, 3, nh)),
            dma((2, nc)),
            dma((2, nc)),
        ],
        compiler_params=pltpu.CompilerParams(collective_id=0, has_side_effects=True, vmem_limit_bytes=52 * 2**20),
        cost_estimate=pl.CostEstimate(
            flops=8 * rows * ex * half, bytes_accessed=2 * (2 * rows * half + ex * feats) + 4 * rows * ex, transcendentals=0),
    )(query, gram, training)
    return raw * weight[None, :]


def by_gathers(query, gram, training, weight):
    whole_gram = lax.all_gather(gram, "ta", axis=1, tiled=True)
    whole_training = lax.all_gather(training, "pb", axis=1, tiled=True)
    mapped = lax.dot_general(
        whole_gram, whole_training, (((1,), (1,)), ((), ())), preferred_element_type=jnp.float32).astype(jnp.bfloat16)
    whole_query = lax.all_gather(query, "ta", axis=1, tiled=True)
    whole_mapped = lax.all_gather(mapped, "pb", axis=0, tiled=True)
    return jnp.dot(whole_query, whole_mapped, preferred_element_type=jnp.float32) * weight[None, :]


def solution(mesh):
    npb, nta, nrow = mesh.shape["pb"], mesh.shape["ta"], mesh.shape["row"]

    def local(query, gram, training, weight):
        ex, feats = training.shape
        square = query.shape == gram.shape == (feats, npb // 2 * feats)
        fits = (
            nta == 2 and nrow == 2 and npb % 4 == 0 and square
            and ex % 128 == 0 and ex >= 384 and feats % 128 == 0)
        if fits:
            return by_kernel(npb, query, gram, training, weight)
        return by_gathers(query, gram, training, weight)

    placed = (P("pb", "ta"), P("pb", "ta"), P(("row", "ta"), "pb"), P(("row", "ta")))
    return jax.shard_map(
        local, mesh=mesh, in_specs=placed, out_specs=P("pb", ("row", "ta")), check_vma=False
    )
```

```python
import functools

import jax
import jax.numpy as jnp
from jax import lax
from jax.experimental import pallas as pl
from jax.experimental.pallas import tpu as pltpu
from jax.sharding import PartitionSpec as P

MESH = pl.DeviceIdType.MESH
SUB = 2
AHEAD = 2


def kernel(npb, nc, q_ref, g_ref, t_ref, out_ref, q_all, g_all, t_all, h_all, kept, part_out, part_in,
           last_out, last_in, own_sem, z_send, z_recv, y_send, y_recv, x_send, x_recv, s_send, s_recv, p_send, p_recv,
           l_send, l_recv):
    me = lax.axis_index("pb")
    ta = lax.axis_index("ta")
    row = lax.axis_index("row")
    nz = npb // 2
    z, y = me // 2, me % 2
    up, down, across = {"pb": me + 2}, {"pb": me - 2}, {"pb": z * 2 + 1 - y}
    xp, sib = {"ta": 1 - ta}, {"row": 1 - row}
    rows, half = g_ref.shape
    ex, feats = t_ref.shape
    width = ex // nc
    nh = half // feats // 2
    strip_rows = rows // 2
    has_up, has_down = z < nz - 1, z > 0

    def remote(src, dst, send_sem, recv_sem, device):
        return pltpu.make_async_remote_copy(
            src_ref=src, dst_ref=dst, send_sem=send_sem, recv_sem=recv_sem, device_id=device, device_id_type=MESH)

    def at(start, size):
        return pl.ds(pl.multiple_of(start * size, size), size)

    def own_columns(which, j, which_y, rows_at):
        return (g_ref, q_ref)[which].at[rows_at, at(j * 2 + which_y, feats)]

    def strip(which, which_y, r, block):
        return (g_all, q_all)[which].at[at(which_y * 2 + r, strip_rows), at(block, feats)]

    own_t = pltpu.make_async_copy(t_ref, t_all.at[z], own_sem.at[0])
    own_t.start()
    own = [
        pltpu.make_async_copy(
            own_columns(which, j, y, pl.ds(0, rows)),
            (g_all, q_all)[which].at[at(y, rows), at(ta * nh + j, feats)], own_sem.at[1 + which * nh + j])
        for which in range(2) for j in range(nh)
    ]

    barrier = pltpu.get_barrier_semaphore()

    def greet(device):
        pl.semaphore_signal(barrier, inc=1, device_id=device, device_id_type=MESH)

    for device in (across, xp, sib):
        greet(device)
    pl.when(has_up)(lambda: greet(up))
    pl.when(has_down)(lambda: greet(down))
    pl.semaphore_wait(barrier, 3 + has_up.astype(jnp.int32) + has_down.astype(jnp.int32))

    def place(phase, c, i, block):
        return (t_all, h_all)[phase].at[block, at(c * SUB + i, width // SUB)]

    def z_copy(phase, c, i, block, way):
        ref = place(phase, c, i, block)
        return remote(ref, ref, z_send.at[phase, c, i, way, block], z_recv.at[phase, c, i, block], (up, down)[way])

    def send_own(phase, c):
        for i in range(SUB):
            pl.when(has_up)(lambda: z_copy(phase, c, i, z, 0).start())
            pl.when(has_down)(lambda: z_copy(phase, c, i, z, 1).start())

    def arrivals(phase, c, pieces=range(SUB)):
        for i in pieces:
            for d in range(1, nz):
                @pl.when(z - d >= 0)
                def _():
                    z_copy(phase, c, i, z - d, 0).wait_recv()
                    pl.when(has_up)(lambda: z_copy(phase, c, i, z - d, 0).start())

                @pl.when(z + d < nz)
                def _():
                    z_copy(phase, c, i, z + d, 1).wait_recv()
                    pl.when(has_down)(lambda: z_copy(phase, c, i, z + d, 1).start())

    def finish_sends(phase, c):
        for i in range(SUB):
            for block in range(nz):
                pl.when(has_up & (block <= z))(lambda: z_copy(phase, c, i, block, 0).wait_send())
                pl.when(has_down & (block >= z))(lambda: z_copy(phase, c, i, block, 1).wait_send())

    def y_out(which, j):
        return remote(
            own_columns(which, j, 1 - y, at(row, strip_rows)), strip(which, y, row, ta * nh + j),
            y_send.at[which, j], y_recv.at[which, j], across)

    def y_in(which, j):
        ref = strip(which, 1 - y, row, ta * nh + j)
        return remote(ref, ref, y_send.at[which, j], y_recv.at[which, j], across)

    def x_out(which, kind, j):
        dst = strip(which, (y, 1 - y)[kind], row, ta * nh + j)
        src = own_columns(which, j, y, at(row, strip_rows)) if kind == 0 else dst
        return remote(src, dst, x_send.at[which, kind, j], x_recv.at[which, kind, j], xp)

    def x_in(which, kind, j):
        ref = strip(which, (y, 1 - y)[kind], row, (1 - ta) * nh + j)
        return remote(ref, ref, x_send.at[which, kind, j], x_recv.at[which, kind, j], xp)

    def s_copy(which, kind, j, r):
        ref = strip(which, (y, 1 - y, 1 - y)[kind], r, (ta if kind == 2 else 1 - ta) * nh + j)
        return remote(ref, ref, s_send.at[which, kind, j], s_recv.at[which, kind, j], sib)

    def from_y(which):
        for j in range(nh):
            y_in(which, j).wait_recv()
            x_out(which, 1, j).start()
            s_copy(which, 2, j, row).start()

    def from_x(which, kind):
        for j in range(nh):
            x_in(which, kind, j).wait_recv()
            s_copy(which, kind, j, row).start()

    def from_sibling(which):
        for kind in range(3):
            for j in range(nh):
                s_copy(which, kind, j, 1 - row).wait_recv()

    def p_copy(phase, c):
        return remote(part_out.at[phase, c], part_in.at[phase, c], p_send.at[phase, c], p_recv.at[phase, c], across)

    def product(left, right, which_y, span):
        examples = jnp.concatenate([right[block, span, :] for block in range(nz)], axis=1)
        return lax.dot_general(
            left[at(which_y, rows), :], examples, (((1,), (1,)), ((), ())), preferred_element_type=jnp.float32)

    def h_partial(c, carry):
        part_out[0, c] = product(g_all, t_all, 1 - y, at(c, width))
        p_copy(0, c).start()
        kept[c] = product(g_all, t_all, y, at(c, width))
        return carry

    def h_combine(c):
        p_copy(0, c).wait_recv()
        h_all[z, at(c, width), :] = (kept[c] + part_in[0, c]).T.astype(jnp.bfloat16)
        send_own(1, c)

    def score_partial(c):
        part_out[1, c] = product(q_all, h_all, 1 - y, at(c, width))
        p_copy(1, c).start()
        out_ref[:, at(c, width)] = product(q_all, h_all, y, at(c, width))

    def score_combine(c):
        p_copy(1, c).wait_recv()
        out_ref[:, at(c, width)] += part_in[1, c]

    small, tall = width // SUB, rows // SUB

    def last_copy(i):
        return remote(last_out.at[i], last_in.at[i], l_send.at[i], l_recv.at[i], across)

    def last_partial(i):
        part = product(q_all, h_all, 1 - y, pl.ds((nc - 1) * width + i * small, small))
        for k in range(SUB):
            last_out[i, :, k * small:(k + 1) * small] = part[k * tall:(k + 1) * tall]
        last_copy(i).start()

    def last_combine(i):
        last_copy(i).wait_recv()
        start = (nc - 1) * width + i * small
        for k in range(SUB):
            out_ref[k * tall:(k + 1) * tall, start:start + small] += last_in[i, :, k * small:(k + 1) * small]

    own_t.wait()
    for c in range(AHEAD):
        send_own(0, c)
    for j in range(nh):
        y_out(0, j).start()
        x_out(0, 0, j).start()
    for copy in own:
        copy.start()

    def step(s, carry):
        pl.when(s + AHEAD < nc)(lambda: send_own(0, s + AHEAD))
        pl.when(s < nc)(lambda: arrivals(0, s))

        @pl.when(s == 0)
        def _():
            from_y(0)
            for j in range(nh):
                y_out(1, j).start()

        @pl.when(s == 1)
        def _():
            from_x(0, 0)

        @pl.when(s == 2)
        def _():
            from_x(0, 1)
            for j in range(nh):
                x_out(1, 0, j).start()
            from_y(1)
            for copy in own:
                copy.wait()
            from_sibling(0)

        lax.fori_loop(jnp.where(s <= 2, 0, s - 1), jnp.where(s < 2, 0, jnp.minimum(s, nc)), h_partial, 0)
        pl.when((s >= 3) & (s < nc + 3))(lambda: h_combine(s - 3))

        @pl.when(s == nc - 1)
        def _():
            from_x(1, 0)

        @pl.when(s >= nc)
        def _():
            c = s - nc

            @pl.when(c == 1)
            def _():
                from_x(1, 1)
                from_sibling(1)

            pl.when(c >= 1)(lambda: score_partial(c - 1))
            pl.when(c < nc - 1)(lambda: arrivals(1, c))
            pl.when(c >= 2)(lambda: score_combine(c - 2))

        return carry

    lax.fori_loop(0, 2 * nc, step, 0)
    for i in range(SUB):
        arrivals(1, nc - 1, [i])
        last_partial(i)
    last = pl.ds((nc - 1) * width, width)
    out_ref[:, last] = product(q_all, h_all, y, last)
    score_combine(nc - 2)
    for i in range(SUB):
        last_combine(i)

    def drain(c, carry):
        for phase in range(2):
            finish_sends(phase, c)
        p_copy(0, c).wait_send()
        pl.when(c < nc - 1)(lambda: p_copy(1, c).wait_send())
        return carry

    lax.fori_loop(0, nc, drain, 0)
    for i in range(SUB):
        last_copy(i).wait_send()
    for which in range(2):
        for j in range(nh):
            y_out(which, j).wait_send()
            for kind in range(2):
                x_out(which, kind, j).wait_send()
            for kind in range(3):
                s_copy(which, kind, j, row).wait_send()


def by_kernel(npb, query, gram, training, weight):
    rows, half = gram.shape
    ex, feats = training.shape
    width = 128
    nc = ex // width
    nz = npb // 2
    nh = half // feats // 2
    anywhere = pl.BlockSpec(memory_space=pl.ANY)
    dma = pltpu.SemaphoreType.DMA
    raw = pl.pallas_call(
        functools.partial(kernel, npb, nc),
        out_shape=jax.ShapeDtypeStruct((rows, ex), jnp.float32),
        in_specs=[anywhere] * 3,
        out_specs=pl.BlockSpec(memory_space=pltpu.VMEM),
        scratch_shapes=[
            pltpu.VMEM((2 * rows, half), jnp.bfloat16),
            pltpu.VMEM((2 * rows, half), jnp.bfloat16),
            pltpu.VMEM((nz, ex, feats), jnp.bfloat16),
            pltpu.VMEM((nz, ex, feats), jnp.bfloat16),
            pltpu.VMEM((nc, rows, width), jnp.float32),
            pltpu.VMEM((2, nc, rows, width), jnp.float32),
            pltpu.VMEM((2, nc, rows, width), jnp.float32),
            pltpu.VMEM((SUB, rows // SUB, width), jnp.float32),
            pltpu.VMEM((SUB, rows // SUB, width), jnp.float32),
            dma((1 + 2 * nh,)),
            dma((2, nc, SUB, 2, nz)),
            dma((2, nc, SUB, nz)),
            dma((2, nh)),
            dma((2, nh)),
            dma((2, 2, nh)),
            dma((2, 2, nh)),
            dma((2, 3, nh)),
            dma((2, 3, nh)),
            dma((2, nc)),
            dma((2, nc)),
            dma((SUB,)),
            dma((SUB,)),
        ],
        compiler_params=pltpu.CompilerParams(collective_id=0, has_side_effects=True, vmem_limit_bytes=52 * 2**20),
        cost_estimate=pl.CostEstimate(
            flops=8 * rows * ex * half, bytes_accessed=2 * (2 * rows * half + ex * feats) + 4 * rows * ex, transcendentals=0),
    )(query, gram, training)
    return raw * weight[None, :]


def by_gathers(query, gram, training, weight):
    whole_gram = lax.all_gather(gram, "ta", axis=1, tiled=True)
    whole_training = lax.all_gather(training, "pb", axis=1, tiled=True)
    mapped = lax.dot_general(
        whole_gram, whole_training, (((1,), (1,)), ((), ())), preferred_element_type=jnp.float32).astype(jnp.bfloat16)
    whole_query = lax.all_gather(query, "ta", axis=1, tiled=True)
    whole_mapped = lax.all_gather(mapped, "pb", axis=0, tiled=True)
    return jnp.dot(whole_query, whole_mapped, preferred_element_type=jnp.float32) * weight[None, :]


def solution(mesh):
    npb, nta, nrow = mesh.shape["pb"], mesh.shape["ta"], mesh.shape["row"]

    def local(query, gram, training, weight):
        ex, feats = training.shape
        square = query.shape == gram.shape == (feats, npb // 2 * feats)
        fits = (
            nta == 2 and nrow == 2 and npb % 4 == 0 and square
            and ex % 128 == 0 and ex >= 384 and feats % 128 == 0)
        if fits:
            return by_kernel(npb, query, gram, training, weight)
        return by_gathers(query, gram, training, weight)

    placed = (P("pb", "ta"), P("pb", "ta"), P(("row", "ta"), "pb"), P(("row", "ta")))
    return jax.shard_map(
        local, mesh=mesh, in_specs=placed, out_specs=P("pb", ("row", "ta")), check_vma=False
    )
```

```python
import functools

import jax
import jax.numpy as jnp
from jax import lax
from jax.experimental import pallas as pl
from jax.experimental.pallas import tpu as pltpu
from jax.sharding import PartitionSpec as P

MESH = pl.DeviceIdType.MESH
SUB = 2


def kernel(npb, nc, q_ref, g_ref, t_ref, out_ref, q_all, g_all, t_all, h_all, turned, kept, part_out, part_in,
           own_sem, z_send, z_recv, y_send, y_recv, x_send, x_recv, s_send, s_recv, p_send, p_recv):
    me = lax.axis_index("pb")
    ta = lax.axis_index("ta")
    row = lax.axis_index("row")
    nz = npb // 2
    z, y = me // 2, me % 2
    up, down, across = {"pb": me + 2}, {"pb": me - 2}, {"pb": z * 2 + 1 - y}
    xp, sib = {"ta": 1 - ta}, {"row": 1 - row}
    rows, half = g_ref.shape
    ex, feats = t_ref.shape
    width = ex // nc
    nh = half // feats // 2
    strip_rows = rows // 2
    has_up, has_down = z < nz - 1, z > 0

    def remote(src, dst, send_sem, recv_sem, device):
        return pltpu.make_async_remote_copy(
            src_ref=src, dst_ref=dst, send_sem=send_sem, recv_sem=recv_sem, device_id=device, device_id_type=MESH)

    def at(start, size):
        return pl.ds(pl.multiple_of(start * size, size), size)

    def own_columns(which, j, which_y, rows_at):
        return (g_ref, q_ref)[which].at[rows_at, at(j * 2 + which_y, feats)]

    def strip(which, which_y, r, block):
        return (g_all, q_all)[which].at[at(which_y * 2 + r, strip_rows), at(block, feats)]

    own_t = pltpu.make_async_copy(t_ref, t_all.at[z], own_sem.at[0])
    own_t.start()
    own = [
        pltpu.make_async_copy(
            own_columns(which, j, y, pl.ds(0, rows)),
            (g_all, q_all)[which].at[at(y, rows), at(ta * nh + j, feats)], own_sem.at[1 + which * nh + j])
        for which in range(2) for j in range(nh)
    ]

    barrier = pltpu.get_barrier_semaphore()

    def greet(device):
        pl.semaphore_signal(barrier, inc=1, device_id=device, device_id_type=MESH)

    for device in (across, xp, sib):
        greet(device)
    pl.when(has_up)(lambda: greet(up))
    pl.when(has_down)(lambda: greet(down))
    pl.semaphore_wait(barrier, 3 + has_up.astype(jnp.int32) + has_down.astype(jnp.int32))

    def place(phase, c, i, block):
        if phase == 0:
            return t_all.at[block, at(c * SUB + i, width // SUB)]
        return h_all.at[c, at(block * SUB + i, rows // SUB)]

    def z_copy(phase, c, i, block, way):
        ref = place(phase, c, i, block)
        return remote(ref, ref, z_send.at[phase, c, i, way, block], z_recv.at[phase, c, i, block], (up, down)[way])

    def send_own(phase, c):
        for i in range(SUB):
            pl.when(has_up)(lambda: z_copy(phase, c, i, z, 0).start())
            pl.when(has_down)(lambda: z_copy(phase, c, i, z, 1).start())

    def arrivals(phase, c):
        for d in range(1, nz):
            for i in range(SUB):
                @pl.when(z - d >= 0)
                def _():
                    z_copy(phase, c, i, z - d, 0).wait_recv()
                    pl.when(has_up)(lambda: z_copy(phase, c, i, z - d, 0).start())

                @pl.when(z + d < nz)
                def _():
                    z_copy(phase, c, i, z + d, 1).wait_recv()
                    pl.when(has_down)(lambda: z_copy(phase, c, i, z + d, 1).start())

    def finish_sends(phase, c):
        for i in range(SUB):
            for block in range(nz):
                pl.when(has_up & (block <= z))(lambda: z_copy(phase, c, i, block, 0).wait_send())
                pl.when(has_down & (block >= z))(lambda: z_copy(phase, c, i, block, 1).wait_send())

    def y_out(which, j):
        return remote(
            own_columns(which, j, 1 - y, at(row, strip_rows)), strip(which, y, row, ta * nh + j),
            y_send.at[which, j], y_recv.at[which, j], across)

    def y_in(which, j):
        ref = strip(which, 1 - y, row, ta * nh + j)
        return remote(ref, ref, y_send.at[which, j], y_recv.at[which, j], across)

    def x_out(which, kind, j):
        dst = strip(which, (y, 1 - y)[kind], row, ta * nh + j)
        src = own_columns(which, j, y, at(row, strip_rows)) if kind == 0 else dst
        return remote(src, dst, x_send.at[which, kind, j], x_recv.at[which, kind, j], xp)

    def x_in(which, kind, j):
        ref = strip(which, (y, 1 - y)[kind], row, (1 - ta) * nh + j)
        return remote(ref, ref, x_send.at[which, kind, j], x_recv.at[which, kind, j], xp)

    def s_copy(which, kind, j, r):
        ref = strip(which, (y, 1 - y, 1 - y)[kind], r, (ta if kind == 2 else 1 - ta) * nh + j)
        return remote(ref, ref, s_send.at[which, kind, j], s_recv.at[which, kind, j], sib)

    def from_y(which):
        for j in range(nh):
            y_in(which, j).wait_recv()
            x_out(which, 1, j).start()
            s_copy(which, 2, j, row).start()

    def from_x(which, kind):
        for j in range(nh):
            x_in(which, kind, j).wait_recv()
            s_copy(which, kind, j, row).start()

    def from_sibling(which):
        for kind in range(3):
            for j in range(nh):
                s_copy(which, kind, j, 1 - row).wait_recv()

    def p_copy(phase, c):
        return remote(part_out.at[phase, c], part_in.at[phase, c], p_send.at[phase, c], p_recv.at[phase, c], across)

    def h_partial(c, carry):
        for block in range(nz):
            turned[block * feats:(block + 1) * feats, :] = t_all[block, at(c, width), :].T

        def product(which_y):
            return jnp.dot(g_all[at(which_y, rows), :], turned[...], preferred_element_type=jnp.float32)

        part_out[0, c] = product(1 - y)
        p_copy(0, c).start()
        kept[c] = product(y)
        return carry

    def h_combine(c):
        p_copy(0, c).wait_recv()
        h_all[c, at(z, rows), :] = (kept[c] + part_in[0, c]).astype(jnp.bfloat16)
        send_own(1, c)

    def score_partial(c):
        def product(which_y):
            return jnp.dot(q_all[at(which_y, rows), :], h_all[c], preferred_element_type=jnp.float32)

        part_out[1, c] = product(1 - y)
        p_copy(1, c).start()
        out_ref[:, at(c, width)] = product(y)

    def score_combine(c):
        p_copy(1, c).wait_recv()
        out_ref[:, at(c, width)] += part_in[1, c]

    own_t.wait()
    send_own(0, 0)
    for j in range(nh):
        y_out(0, j).start()
        x_out(0, 0, j).start()
    for copy in own:
        copy.start()

    def step(s, carry):
        pl.when(s + 1 < nc)(lambda: send_own(0, s + 1))
        pl.when(s < nc)(lambda: arrivals(0, s))

        @pl.when(s == 0)
        def _():
            from_y(0)
            for j in range(nh):
                y_out(1, j).start()

        @pl.when(s == 1)
        def _():
            from_x(0, 0)

        @pl.when(s == 2)
        def _():
            from_x(0, 1)
            for j in range(nh):
                x_out(1, 0, j).start()
            from_y(1)
            for copy in own:
                copy.wait()
            from_sibling(0)

        lax.fori_loop(jnp.where(s <= 2, 0, s - 1), jnp.where(s < 2, 0, jnp.minimum(s, nc)), h_partial, 0)
        pl.when((s >= 3) & (s < nc + 3))(lambda: h_combine(s - 3))

        @pl.when(s == nc - 1)
        def _():
            from_x(1, 0)

        @pl.when(s >= nc)
        def _():
            c = s - nc

            @pl.when(c == 1)
            def _():
                from_x(1, 1)
                from_sibling(1)

            pl.when(c >= 1)(lambda: score_partial(c - 1))
            arrivals(1, c)
            pl.when(c >= 2)(lambda: score_combine(c - 2))

        return carry

    lax.fori_loop(0, 2 * nc, step, 0)
    score_partial(nc - 1)
    score_combine(nc - 2)
    score_combine(nc - 1)

    def drain(c, carry):
        for phase in range(2):
            finish_sends(phase, c)
            p_copy(phase, c).wait_send()
        return carry

    lax.fori_loop(0, nc, drain, 0)
    for which in range(2):
        for j in range(nh):
            y_out(which, j).wait_send()
            for kind in range(2):
                x_out(which, kind, j).wait_send()
            for kind in range(3):
                s_copy(which, kind, j, row).wait_send()


def by_kernel(npb, query, gram, training, weight):
    rows, half = gram.shape
    ex, feats = training.shape
    width = 128
    nc = ex // width
    nz = npb // 2
    nh = half // feats // 2
    anywhere = pl.BlockSpec(memory_space=pl.ANY)
    dma = pltpu.SemaphoreType.DMA
    raw = pl.pallas_call(
        functools.partial(kernel, npb, nc),
        out_shape=jax.ShapeDtypeStruct((rows, ex), jnp.float32),
        in_specs=[anywhere] * 3,
        out_specs=pl.BlockSpec(memory_space=pltpu.VMEM),
        scratch_shapes=[
            pltpu.VMEM((2 * rows, half), jnp.bfloat16),
            pltpu.VMEM((2 * rows, half), jnp.bfloat16),
            pltpu.VMEM((nz, ex, feats), jnp.bfloat16),
            pltpu.VMEM((nc, half, width), jnp.bfloat16),
            pltpu.VMEM((half, width), jnp.bfloat16),
            pltpu.VMEM((nc, rows, width), jnp.float32),
            pltpu.VMEM((2, nc, rows, width), jnp.float32),
            pltpu.VMEM((2, nc, rows, width), jnp.float32),
            dma((1 + 2 * nh,)),
            dma((2, nc, SUB, 2, nz)),
            dma((2, nc, SUB, nz)),
            dma((2, nh)),
            dma((2, nh)),
            dma((2, 2, nh)),
            dma((2, 2, nh)),
            dma((2, 3, nh)),
            dma((2, 3, nh)),
            dma((2, nc)),
            dma((2, nc)),
        ],
        compiler_params=pltpu.CompilerParams(collective_id=0, has_side_effects=True, vmem_limit_bytes=52 * 2**20),
        cost_estimate=pl.CostEstimate(
            flops=8 * rows * ex * half, bytes_accessed=2 * (2 * rows * half + ex * feats) + 4 * rows * ex, transcendentals=0),
    )(query, gram, training)
    return raw * weight[None, :]


def by_gathers(query, gram, training, weight):
    whole_gram = lax.all_gather(gram, "ta", axis=1, tiled=True)
    whole_training = lax.all_gather(training, "pb", axis=1, tiled=True)
    mapped = lax.dot_general(
        whole_gram, whole_training, (((1,), (1,)), ((), ())), preferred_element_type=jnp.float32).astype(jnp.bfloat16)
    whole_query = lax.all_gather(query, "ta", axis=1, tiled=True)
    whole_mapped = lax.all_gather(mapped, "pb", axis=0, tiled=True)
    return jnp.dot(whole_query, whole_mapped, preferred_element_type=jnp.float32) * weight[None, :]


def solution(mesh):
    npb, nta, nrow = mesh.shape["pb"], mesh.shape["ta"], mesh.shape["row"]

    def local(query, gram, training, weight):
        ex, feats = training.shape
        square = query.shape == gram.shape == (feats, npb // 2 * feats)
        fits = (
            nta == 2 and nrow == 2 and npb % 4 == 0 and square
            and ex % 128 == 0 and ex >= 384 and feats % 128 == 0)
        if fits:
            return by_kernel(npb, query, gram, training, weight)
        return by_gathers(query, gram, training, weight)

    placed = (P("pb", "ta"), P("pb", "ta"), P(("row", "ta"), "pb"), P(("row", "ta")))
    return jax.shard_map(
        local, mesh=mesh, in_specs=placed, out_specs=P("pb", ("row", "ta")), check_vma=False
    )
```

```python
import functools

import jax
import jax.numpy as jnp
from jax import lax
from jax.experimental import pallas as pl
from jax.experimental.pallas import tpu as pltpu
from jax.sharding import PartitionSpec as P

MESH = pl.DeviceIdType.MESH
SUB = 2

ORDER = (
    (
        ("own", 0, 0, 0), ("over_x", 0, 1), ("own", 0, 3, 1), ("own", 0, 1, 0), ("over_y", 0, 1),
        ("pass_on", 0, 3, 1, 1), ("pass_on", 0, 1, 1, 0), ("pass_on", 0, 0, 1, 0), ("over_x", 0, 0),
        ("over_y", 0, 0), ("own", 0, 3, 0), ("from_y", 0, 1), ("from_x", 0, 0, 1), ("own", 0, 2, 1),
        ("over_y", 1, 1), ("own", 0, 0, 1), ("pass_on", 0, 0, 2, 0), ("pass_on", 0, 1, 2, 0), ("from_y", 0, 0),
        ("own", 0, 1, 1), ("from_x", 0, 0, 0), ("over_y", 1, 0), ("pass_on", 0, 0, 1, 1), ("from_x", 0, 1, 1),
        ("own", 0, 2, 0), ("pass_on", 0, 0, 2, 1), ("pass_on", 0, 1, 1, 1), ("from_x", 0, 1, 0),
        ("pass_on", 0, 1, 2, 1), ("pass_on", 0, 1, 3, 0), ("pass_on", 0, 0, 3, 1), ("pass_on", 0, 3, 1, 0),
        ("over_x", 1, 0), ("sibling", 0), ("pass_on", 0, 2, 1, 1), ("pass_on", 0, 0, 3, 0), ("from_y", 1, 0),
        ("pass_on", 0, 2, 1, 0),
    ),
    (
        ("pass_on", 0, 3, 2, 1), ("pass_on", 0, 2, 2, 1), ("pass_on", 0, 1, 3, 1), ("pass_on", 0, 2, 2, 0),
        ("pass_on", 0, 3, 2, 0),
    ),
    (
        ("h_sum", 0), ("own", 1, 0, 1), ("pass_on", 0, 3, 3, 1), ("pass_on", 0, 2, 3, 1), ("own", 1, 0, 0),
        ("from_y", 1, 1), ("pass_on", 0, 2, 3, 0),
    ),
    (
        ("pass_on", 1, 0, 1, 1), ("h_sum", 1), ("over_x", 1, 1), ("own", 1, 1, 1), ("from_x", 1, 1, 0),
        ("own", 1, 1, 0), ("pass_on", 1, 0, 1, 0), ("pass_on", 0, 3, 3, 0),
    ),
    (
        ("pass_on", 1, 0, 2, 1), ("pass_on", 1, 1, 1, 1), ("from_x", 1, 0, 0), ("pass_on", 1, 1, 1, 0),
        ("h_sum", 2), ("pass_on", 1, 0, 3, 1), ("from_x", 1, 1, 1), ("from_x", 1, 0, 1), ("pass_on", 1, 0, 2, 0),
        ("pass_on", 1, 1, 2, 0), ("pass_on", 1, 1, 2, 1), ("sibling", 1), ("own", 1, 2, 1), ("own", 1, 2, 0),
        ("h_sum", 3), ("pass_on", 1, 0, 3, 0),
    ),
    (
        ("pass_on", 1, 1, 3, 1), ("pass_on", 1, 1, 3, 0), ("own", 1, 3, 0), ("pass_on", 1, 2, 1, 0),
        ("own", 1, 3, 1), ("pass_on", 1, 2, 1, 1),
    ),
    (
        ("pass_on", 1, 2, 2, 1), ("pass_on", 1, 2, 2, 0), ("pass_on", 1, 2, 3, 0), ("pass_on", 1, 2, 3, 1),
    ),
    (
        ("pass_on", 1, 3, 1, 1), ("score_sum", 1), ("pass_on", 1, 3, 1, 0), ("pass_on", 1, 3, 3, 1),
        ("pass_on", 1, 3, 2, 1), ("pass_on", 1, 3, 3, 0), ("pass_on", 1, 3, 2, 0),
    ),
    (
        ("score_sum", 2), ("score_sum", 0), ("score_sum", 3),
    ),
)


def kernel(npb, nc, q_ref, g_ref, t_ref, out_ref, q_all, g_all, t_all, h_all, turned, kept, part_out, part_in,
           own_sem, z_send, z_recv, y_send, y_recv, x_send, x_recv, s_send, s_recv, p_send, p_recv):
    me = lax.axis_index("pb")
    ta = lax.axis_index("ta")
    row = lax.axis_index("row")
    nz = npb // 2
    z, y = me // 2, me % 2
    up, down, across = {"pb": me + 2}, {"pb": me - 2}, {"pb": z * 2 + 1 - y}
    xp, sib = {"ta": 1 - ta}, {"row": 1 - row}
    rows, half = g_ref.shape
    ex, feats = t_ref.shape
    width = ex // nc
    nh = half // feats // 2
    strip_rows = rows // 2
    has_up, has_down = z < nz - 1, z > 0

    def remote(src, dst, send_sem, recv_sem, device):
        return pltpu.make_async_remote_copy(
            src_ref=src, dst_ref=dst, send_sem=send_sem, recv_sem=recv_sem, device_id=device, device_id_type=MESH)

    def at(start, size):
        return pl.ds(pl.multiple_of(start * size, size), size)

    def own_columns(which, j, which_y, rows_at):
        return (g_ref, q_ref)[which].at[rows_at, at(j * 2 + which_y, feats)]

    def strip(which, which_y, r, block):
        return (g_all, q_all)[which].at[at(which_y * 2 + r, strip_rows), at(block, feats)]

    own_t = pltpu.make_async_copy(t_ref, t_all.at[z], own_sem.at[0])
    own_t.start()
    own = [
        pltpu.make_async_copy(
            own_columns(which, j, y, pl.ds(0, rows)),
            (g_all, q_all)[which].at[at(y, rows), at(ta * nh + j, feats)], own_sem.at[1 + which * nh + j])
        for which in range(2) for j in range(nh)
    ]
    for copy in own:
        copy.start()

    barrier = pltpu.get_barrier_semaphore()

    def greet(device):
        pl.semaphore_signal(barrier, inc=1, device_id=device, device_id_type=MESH)

    for device in (across, xp, sib):
        greet(device)
    pl.when(has_up)(lambda: greet(up))
    pl.when(has_down)(lambda: greet(down))
    pl.semaphore_wait(barrier, 3 + has_up.astype(jnp.int32) + has_down.astype(jnp.int32))

    def place(phase, c, i, block):
        if phase == 0:
            return t_all.at[block, at(c * SUB + i, width // SUB)]
        return h_all.at[c, at(block * SUB + i, rows // SUB)]

    def z_copy(phase, c, i, block, way):
        ref = place(phase, c, i, block)
        return remote(ref, ref, z_send.at[phase, c, i, way, block], z_recv.at[phase, c, i, block], (up, down)[way])

    def send_own(phase, c, i):
        pl.when(has_up)(lambda: z_copy(phase, c, i, z, 0).start())
        pl.when(has_down)(lambda: z_copy(phase, c, i, z, 1).start())

    def pass_on(phase, c, d, i):
        @pl.when(z - d >= 0)
        def _():
            z_copy(phase, c, i, z - d, 0).wait_recv()
            pl.when(has_up)(lambda: z_copy(phase, c, i, z - d, 0).start())

        @pl.when(z + d < nz)
        def _():
            z_copy(phase, c, i, z + d, 1).wait_recv()
            pl.when(has_down)(lambda: z_copy(phase, c, i, z + d, 1).start())

    def finish_sends(phase, c):
        for i in range(SUB):
            for block in range(nz):
                pl.when(has_up & (block <= z))(lambda: z_copy(phase, c, i, block, 0).wait_send())
                pl.when(has_down & (block >= z))(lambda: z_copy(phase, c, i, block, 1).wait_send())

    def y_out(which, j):
        return remote(
            own_columns(which, j, 1 - y, at(row, strip_rows)), strip(which, y, row, ta * nh + j),
            y_send.at[which, j], y_recv.at[which, j], across)

    def y_in(which, j):
        ref = strip(which, 1 - y, row, ta * nh + j)
        return remote(ref, ref, y_send.at[which, j], y_recv.at[which, j], across)

    def x_out(which, kind, j):
        dst = strip(which, (y, 1 - y)[kind], row, ta * nh + j)
        src = own_columns(which, j, y, at(row, strip_rows)) if kind == 0 else dst
        return remote(src, dst, x_send.at[which, kind, j], x_recv.at[which, kind, j], xp)

    def x_in(which, kind, j):
        ref = strip(which, (y, 1 - y)[kind], row, (1 - ta) * nh + j)
        return remote(ref, ref, x_send.at[which, kind, j], x_recv.at[which, kind, j], xp)

    def s_copy(which, kind, j, r):
        ref = strip(which, (y, 1 - y, 1 - y)[kind], r, (ta if kind == 2 else 1 - ta) * nh + j)
        return remote(ref, ref, s_send.at[which, kind, j], s_recv.at[which, kind, j], sib)

    def from_y(which, j):
        y_in(which, j).wait_recv()
        x_out(which, 1, j).start()
        s_copy(which, 2, j, row).start()

    def from_x(which, kind, j):
        x_in(which, kind, j).wait_recv()
        s_copy(which, kind, j, row).start()

    def from_sibling(which):
        for kind in range(3):
            for j in range(nh):
                s_copy(which, kind, j, 1 - row).wait_recv()
        for copy in own[which * nh:(which + 1) * nh]:
            copy.wait()

    def p_copy(phase, c):
        return remote(part_out.at[phase, c], part_in.at[phase, c], p_send.at[phase, c], p_recv.at[phase, c], across)

    def h_partial(c):
        for block in range(nz):
            turned[block * feats:(block + 1) * feats, :] = t_all[block, at(c, width), :].T

        def product(which_y):
            return jnp.dot(g_all[at(which_y, rows), :], turned[...], preferred_element_type=jnp.float32)

        part_out[0, c] = product(1 - y)
        p_copy(0, c).start()
        kept[c] = product(y)

    def h_combine(c):
        p_copy(0, c).wait_recv()
        h_all[c, at(z, rows), :] = (kept[c] + part_in[0, c]).astype(jnp.bfloat16)

    def score_partial(c):
        def product(which_y):
            return jnp.dot(q_all[at(which_y, rows), :], h_all[c], preferred_element_type=jnp.float32)

        part_out[1, c] = product(1 - y)
        p_copy(1, c).start()
        out_ref[:, at(c, width)] = product(y)

    def score_combine(c):
        p_copy(1, c).wait_recv()
        out_ref[:, at(c, width)] += part_in[1, c]

    own_t.wait()
    steps = {
        "own": send_own, "pass_on": pass_on, "over_y": lambda which, j: y_out(which, j).start(),
        "over_x": lambda which, j: x_out(which, 0, j).start(), "from_y": from_y, "from_x": from_x,
        "sibling": from_sibling, "h_sum": h_combine, "score_sum": score_combine,
    }

    def stage(s, carry):
        for k, group in enumerate(ORDER):
            @pl.when(s == k)
            def _():
                for name, *which in group:
                    steps[name](*which)

        pl.when(s < nc)(lambda: h_partial(s))
        pl.when((s >= nc) & (s < 2 * nc))(lambda: score_partial(s - nc))
        return carry

    lax.fori_loop(0, 2 * nc + 1, stage, 0)

    def drain(c, carry):
        for phase in range(2):
            finish_sends(phase, c)
            p_copy(phase, c).wait_send()
        return carry

    lax.fori_loop(0, nc, drain, 0)
    for which in range(2):
        for j in range(nh):
            y_out(which, j).wait_send()
            for kind in range(2):
                x_out(which, kind, j).wait_send()
            for kind in range(3):
                s_copy(which, kind, j, row).wait_send()


def by_kernel(npb, query, gram, training, weight):
    rows, half = gram.shape
    ex, feats = training.shape
    width = 128
    nc = ex // width
    nz = npb // 2
    nh = half // feats // 2
    anywhere = pl.BlockSpec(memory_space=pl.ANY)
    dma = pltpu.SemaphoreType.DMA
    raw = pl.pallas_call(
        functools.partial(kernel, npb, nc),
        out_shape=jax.ShapeDtypeStruct((rows, ex), jnp.float32),
        in_specs=[anywhere] * 3,
        out_specs=pl.BlockSpec(memory_space=pltpu.VMEM),
        scratch_shapes=[
            pltpu.VMEM((2 * rows, half), jnp.bfloat16),
            pltpu.VMEM((2 * rows, half), jnp.bfloat16),
            pltpu.VMEM((nz, ex, feats), jnp.bfloat16),
            pltpu.VMEM((nc, half, width), jnp.bfloat16),
            pltpu.VMEM((half, width), jnp.bfloat16),
            pltpu.VMEM((nc, rows, width), jnp.float32),
            pltpu.VMEM((2, nc, rows, width), jnp.float32),
            pltpu.VMEM((2, nc, rows, width), jnp.float32),
            dma((1 + 2 * nh,)),
            dma((2, nc, SUB, 2, nz)),
            dma((2, nc, SUB, nz)),
            dma((2, nh)),
            dma((2, nh)),
            dma((2, 2, nh)),
            dma((2, 2, nh)),
            dma((2, 3, nh)),
            dma((2, 3, nh)),
            dma((2, nc)),
            dma((2, nc)),
        ],
        compiler_params=pltpu.CompilerParams(collective_id=0, has_side_effects=True, vmem_limit_bytes=52 * 2**20),
        cost_estimate=pl.CostEstimate(
            flops=8 * rows * ex * half, bytes_accessed=2 * (2 * rows * half + ex * feats) + 4 * rows * ex, transcendentals=0),
    )(query, gram, training)
    return raw * weight[None, :]


def by_gathers(query, gram, training, weight):
    whole_gram = lax.all_gather(gram, "ta", axis=1, tiled=True)
    whole_training = lax.all_gather(training, "pb", axis=1, tiled=True)
    mapped = lax.dot_general(
        whole_gram, whole_training, (((1,), (1,)), ((), ())), preferred_element_type=jnp.float32).astype(jnp.bfloat16)
    whole_query = lax.all_gather(query, "ta", axis=1, tiled=True)
    whole_mapped = lax.all_gather(mapped, "pb", axis=0, tiled=True)
    return jnp.dot(whole_query, whole_mapped, preferred_element_type=jnp.float32) * weight[None, :]


def solution(mesh):
    npb, nta, nrow = mesh.shape["pb"], mesh.shape["ta"], mesh.shape["row"]

    def local(query, gram, training, weight):
        ex, feats = training.shape
        square = query.shape == gram.shape == (feats, npb // 2 * feats)
        fits = (
            nta == 2 and nrow == 2 and npb == 8 and square and ex == 512 and feats % 128 == 0)
        if fits:
            return by_kernel(npb, query, gram, training, weight)
        return by_gathers(query, gram, training, weight)

    placed = (P("pb", "ta"), P("pb", "ta"), P(("row", "ta"), "pb"), P(("row", "ta")))
    return jax.shard_map(
        local, mesh=mesh, in_specs=placed, out_specs=P("pb", ("row", "ta")), check_vma=False
    )
```

```python
import functools

import jax
import jax.numpy as jnp
from jax import lax
from jax.experimental import pallas as pl
from jax.experimental.pallas import tpu as pltpu
from jax.sharding import PartitionSpec as P

MESH = pl.DeviceIdType.MESH
SUB = 2

ORDER = (
    (
        ("over_x", 0, 1), ("over_y", 0, 1), ("own", 0, 0, 1), ("own", 0, 3, 1), ("own", 0, 1, 0), ("own", 0, 2, 1),
        ("over_x", 0, 0), ("pass_on", 0, 0, 1, 1), ("from_y", 0, 1), ("over_y", 0, 0), ("pass_on", 0, 3, 1, 1),
        ("pass_on", 0, 1, 1, 0), ("pass_on", 0, 1, 2, 0), ("over_y", 1, 0), ("own", 0, 3, 0), ("own", 0, 1, 1),
        ("from_x", 0, 0, 0), ("own", 0, 0, 0), ("from_y", 0, 0), ("own", 0, 2, 0), ("over_y", 1, 1),
        ("pass_on", 0, 0, 1, 0), ("pass_on", 0, 0, 2, 1), ("from_x", 0, 1, 1), ("from_x", 0, 0, 1),
        ("pass_on", 0, 0, 2, 0), ("pass_on", 0, 1, 1, 1), ("from_x", 0, 1, 0), ("pass_on", 0, 2, 1, 0),
        ("pass_on", 0, 1, 3, 0), ("over_x", 1, 1), ("sibling", 0), ("pass_on", 0, 1, 2, 1),
        ("pass_on", 0, 0, 3, 0), ("pass_on", 0, 2, 1, 1), ("pass_on", 0, 3, 1, 0), ("from_y", 1, 0),
        ("pass_on", 0, 0, 3, 1),
    ),
    (
        ("pass_on", 0, 1, 3, 1), ("pass_on", 0, 2, 2, 0), ("from_y", 1, 1), ("pass_on", 0, 3, 2, 0),
        ("pass_on", 0, 2, 2, 1),
    ),
    (
        ("pass_on", 0, 3, 2, 1), ("h_sum", 0), ("pass_on", 0, 2, 3, 0), ("own", 1, 0, 0), ("pass_on", 0, 3, 3, 1),
        ("pass_on", 0, 2, 3, 1), ("own", 1, 0, 1),
    ),
    (
        ("pass_on", 1, 0, 1, 0), ("pass_on", 1, 0, 1, 1), ("pass_on", 0, 3, 3, 0), ("from_x", 1, 0, 1),
        ("h_sum", 1), ("own", 1, 1, 0), ("own", 1, 1, 1), ("over_x", 1, 0),
    ),
    (
        ("pass_on", 1, 0, 2, 0), ("pass_on", 1, 1, 1, 1), ("pass_on", 1, 0, 2, 1), ("pass_on", 1, 1, 1, 0),
        ("h_sum", 2), ("from_x", 1, 1, 1), ("own", 1, 2, 1), ("from_x", 1, 1, 0), ("from_x", 1, 0, 0),
        ("pass_on", 1, 1, 2, 0), ("pass_on", 1, 0, 3, 1), ("sibling", 1), ("own", 1, 2, 0), ("h_sum", 3),
        ("pass_on", 1, 2, 1, 1), ("pass_on", 1, 1, 2, 1), ("pass_on", 1, 0, 3, 0),
    ),
    (
        ("pass_on", 1, 1, 3, 0), ("pass_on", 1, 1, 3, 1), ("own", 1, 3, 0), ("pass_on", 1, 2, 1, 0),
    ),
    (
        ("pass_on", 1, 2, 2, 0), ("pass_on", 1, 2, 2, 1), ("own", 1, 3, 1), ("pass_on", 1, 2, 3, 0),
        ("pass_on", 1, 2, 3, 1),
    ),
    (
        ("pass_on", 1, 3, 1, 0), ("pass_on", 1, 3, 1, 1), ("pass_on", 1, 3, 2, 0), ("pass_on", 1, 3, 3, 0),
        ("last_half", 0), ("pass_on", 1, 3, 3, 1), ("pass_on", 1, 3, 2, 1), ("last_half", 1), ("score_sum", 2),
        ("score_sum", 1), ("score_sum", 0), ("score_sum", 3),
    ),
)


def kernel(npb, nc, q_ref, g_ref, t_ref, out_ref, q_all, g_all, t_all, h_all, turned, kept, part_out, part_in,
           last_out, last_in, own_sem, z_send, z_recv, y_send, y_recv, x_send, x_recv, s_send, s_recv, p_send, p_recv, l_send, l_recv):
    me = lax.axis_index("pb")
    ta = lax.axis_index("ta")
    row = lax.axis_index("row")
    nz = npb // 2
    z, y = me // 2, me % 2
    up, down, across = {"pb": me + 2}, {"pb": me - 2}, {"pb": z * 2 + 1 - y}
    xp, sib = {"ta": 1 - ta}, {"row": 1 - row}
    rows, half = g_ref.shape
    ex, feats = t_ref.shape
    width = ex // nc
    nh = half // feats // 2
    strip_rows = rows // 2
    has_up, has_down = z < nz - 1, z > 0

    def remote(src, dst, send_sem, recv_sem, device):
        return pltpu.make_async_remote_copy(
            src_ref=src, dst_ref=dst, send_sem=send_sem, recv_sem=recv_sem, device_id=device, device_id_type=MESH)

    def at(start, size):
        return pl.ds(pl.multiple_of(start * size, size), size)

    def own_columns(which, j, which_y, rows_at):
        return (g_ref, q_ref)[which].at[rows_at, at(j * 2 + which_y, feats)]

    def strip(which, which_y, r, block):
        return (g_all, q_all)[which].at[at(which_y * 2 + r, strip_rows), at(block, feats)]

    own_t = pltpu.make_async_copy(t_ref, t_all.at[z], own_sem.at[0])
    own_t.start()
    own = [
        pltpu.make_async_copy(
            own_columns(which, j, y, pl.ds(0, rows)),
            (g_all, q_all)[which].at[at(y, rows), at(ta * nh + j, feats)], own_sem.at[1 + which * nh + j])
        for which in range(2) for j in range(nh)
    ]
    for copy in own:
        copy.start()

    barrier = pltpu.get_barrier_semaphore()

    def greet(device):
        pl.semaphore_signal(barrier, inc=1, device_id=device, device_id_type=MESH)

    for device in (across, xp, sib):
        greet(device)
    pl.when(has_up)(lambda: greet(up))
    pl.when(has_down)(lambda: greet(down))
    pl.semaphore_wait(barrier, 3 + has_up.astype(jnp.int32) + has_down.astype(jnp.int32))

    def place(phase, c, i, block):
        if phase == 0:
            return t_all.at[block, at(c * SUB + i, width // SUB)]
        return h_all.at[c, at(block * SUB + i, rows // SUB)]

    def z_copy(phase, c, i, block, way):
        ref = place(phase, c, i, block)
        return remote(ref, ref, z_send.at[phase, c, i, way, block], z_recv.at[phase, c, i, block], (up, down)[way])

    def send_own(phase, c, i):
        pl.when(has_up)(lambda: z_copy(phase, c, i, z, 0).start())
        pl.when(has_down)(lambda: z_copy(phase, c, i, z, 1).start())

    def pass_on(phase, c, d, i):
        @pl.when(z - d >= 0)
        def _():
            z_copy(phase, c, i, z - d, 0).wait_recv()
            pl.when(has_up)(lambda: z_copy(phase, c, i, z - d, 0).start())

        @pl.when(z + d < nz)
        def _():
            z_copy(phase, c, i, z + d, 1).wait_recv()
            pl.when(has_down)(lambda: z_copy(phase, c, i, z + d, 1).start())

    def finish_sends(phase, c):
        for i in range(SUB):
            for block in range(nz):
                pl.when(has_up & (block <= z))(lambda: z_copy(phase, c, i, block, 0).wait_send())
                pl.when(has_down & (block >= z))(lambda: z_copy(phase, c, i, block, 1).wait_send())

    def y_out(which, j):
        return remote(
            own_columns(which, j, 1 - y, at(row, strip_rows)), strip(which, y, row, ta * nh + j),
            y_send.at[which, j], y_recv.at[which, j], across)

    def y_in(which, j):
        ref = strip(which, 1 - y, row, ta * nh + j)
        return remote(ref, ref, y_send.at[which, j], y_recv.at[which, j], across)

    def x_out(which, kind, j):
        dst = strip(which, (y, 1 - y)[kind], row, ta * nh + j)
        src = own_columns(which, j, y, at(row, strip_rows)) if kind == 0 else dst
        return remote(src, dst, x_send.at[which, kind, j], x_recv.at[which, kind, j], xp)

    def x_in(which, kind, j):
        ref = strip(which, (y, 1 - y)[kind], row, (1 - ta) * nh + j)
        return remote(ref, ref, x_send.at[which, kind, j], x_recv.at[which, kind, j], xp)

    def s_copy(which, kind, j, r):
        ref = strip(which, (y, 1 - y, 1 - y)[kind], r, (ta if kind == 2 else 1 - ta) * nh + j)
        return remote(ref, ref, s_send.at[which, kind, j], s_recv.at[which, kind, j], sib)

    def from_y(which, j):
        y_in(which, j).wait_recv()
        x_out(which, 1, j).start()
        s_copy(which, 2, j, row).start()

    def from_x(which, kind, j):
        x_in(which, kind, j).wait_recv()
        s_copy(which, kind, j, row).start()

    def from_sibling(which):
        for kind in range(3):
            for j in range(nh):
                s_copy(which, kind, j, 1 - row).wait_recv()
        for copy in own[which * nh:(which + 1) * nh]:
            copy.wait()

    def p_copy(phase, c):
        return remote(part_out.at[phase, c], part_in.at[phase, c], p_send.at[phase, c], p_recv.at[phase, c], across)

    tall = rows // 2
    left_lanes = lax.broadcasted_iota(jnp.int32, (tall, width), 1) < width // 2
    last = pl.ds((nc - 1) * width, width)

    def swap_quarters(one, two):
        turn = lambda x: pltpu.roll(x, width // 2, 1)
        return [jnp.where(left_lanes, one, turn(two)), jnp.where(left_lanes, turn(one), two)]

    def last_copy(i):
        return remote(last_out.at[i], last_in.at[i], l_send.at[i], l_recv.at[i], across)

    def last_product(which_y, i):
        sums = []
        for k in range(2):
            sums.append(sum(
                jnp.dot(q_all[at(which_y, rows), block * feats + k * tall:block * feats + (k + 1) * tall],
                        h_all[nc - 1, (block * 2 + i) * tall:(block * 2 + i + 1) * tall, :],
                        preferred_element_type=jnp.float32)
                for block in range(nz)))
        return sums[0] + pltpu.roll(sums[1], width // 2, 1)

    def last_half(i):
        part = last_product(1 - y, i)
        last_out[i] = swap_quarters(part[:tall], part[tall:])[0]
        last_copy(i).start()
        part = last_product(y, i)
        if i == 0:
            out_ref[:, last] = part
        else:
            both = jnp.concatenate([left_lanes, left_lanes], axis=0)
            out_ref[:, last] = jnp.where(both, out_ref[:, last], pltpu.roll(part, width // 2, 1))

    def last_combine():
        for i in range(2):
            last_copy(i).wait_recv()
        upper, lower = swap_quarters(last_in[0], last_in[1])
        out_ref[:tall, last] += upper
        out_ref[tall:, last] += lower

    def h_partial(c):
        for block in range(nz):
            turned[block * feats:(block + 1) * feats, :] = t_all[block, at(c, width), :].T

        def product(which_y):
            return jnp.dot(g_all[at(which_y, rows), :], turned[...], preferred_element_type=jnp.float32)

        part_out[0, c] = product(1 - y)
        p_copy(0, c).start()
        kept[c] = product(y)

    def h_combine(c):
        p_copy(0, c).wait_recv()
        h = kept[c] + part_in[0, c]
        if c == nc - 1:
            h = jnp.concatenate(swap_quarters(h[:tall], h[tall:]), axis=0)
        h_all[c, at(z, rows), :] = h.astype(jnp.bfloat16)

    def score_partial(c):
        def product(which_y):
            return jnp.dot(q_all[at(which_y, rows), :], h_all[c], preferred_element_type=jnp.float32)

        part_out[1, c] = product(1 - y)
        p_copy(1, c).start()
        out_ref[:, at(c, width)] = product(y)

    def score_combine(c):
        if c == nc - 1:
            return last_combine()
        p_copy(1, c).wait_recv()
        out_ref[:, at(c, width)] += part_in[1, c]

    own_t.wait()
    steps = {
        "own": send_own, "pass_on": pass_on, "over_y": lambda which, j: y_out(which, j).start(),
        "over_x": lambda which, j: x_out(which, 0, j).start(), "from_y": from_y, "from_x": from_x,
        "sibling": from_sibling, "h_sum": h_combine, "score_sum": score_combine, "last_half": last_half,
    }

    def stage(s, carry):
        for k, group in enumerate(ORDER):
            @pl.when(s == k)
            def _():
                for name, *which in group:
                    steps[name](*which)

        pl.when(s < nc)(lambda: h_partial(s))
        pl.when((s >= nc) & (s < 2 * nc - 1))(lambda: score_partial(s - nc))
        return carry

    lax.fori_loop(0, 2 * nc, stage, 0)

    def drain(c, carry):
        for phase in range(2):
            finish_sends(phase, c)
        p_copy(0, c).wait_send()
        pl.when(c < nc - 1)(lambda: p_copy(1, c).wait_send())
        return carry

    lax.fori_loop(0, nc, drain, 0)
    for i in range(2):
        last_copy(i).wait_send()
    for which in range(2):
        for j in range(nh):
            y_out(which, j).wait_send()
            for kind in range(2):
                x_out(which, kind, j).wait_send()
            for kind in range(3):
                s_copy(which, kind, j, row).wait_send()


def by_kernel(npb, query, gram, training, weight):
    rows, half = gram.shape
    ex, feats = training.shape
    width = 128
    nc = ex // width
    nz = npb // 2
    nh = half // feats // 2
    anywhere = pl.BlockSpec(memory_space=pl.ANY)
    dma = pltpu.SemaphoreType.DMA
    raw = pl.pallas_call(
        functools.partial(kernel, npb, nc),
        out_shape=jax.ShapeDtypeStruct((rows, ex), jnp.float32),
        in_specs=[anywhere] * 3,
        out_specs=pl.BlockSpec(memory_space=pltpu.VMEM),
        scratch_shapes=[
            pltpu.VMEM((2 * rows, half), jnp.bfloat16),
            pltpu.VMEM((2 * rows, half), jnp.bfloat16),
            pltpu.VMEM((nz, ex, feats), jnp.bfloat16),
            pltpu.VMEM((nc, half, width), jnp.bfloat16),
            pltpu.VMEM((half, width), jnp.bfloat16),
            pltpu.VMEM((nc, rows, width), jnp.float32),
            pltpu.VMEM((2, nc, rows, width), jnp.float32),
            pltpu.VMEM((2, nc, rows, width), jnp.float32),
            pltpu.VMEM((2, rows // 2, width), jnp.float32),
            pltpu.VMEM((2, rows // 2, width), jnp.float32),
            dma((1 + 2 * nh,)),
            dma((2, nc, SUB, 2, nz)),
            dma((2, nc, SUB, nz)),
            dma((2, nh)),
            dma((2, nh)),
            dma((2, 2, nh)),
            dma((2, 2, nh)),
            dma((2, 3, nh)),
            dma((2, 3, nh)),
            dma((2, nc)),
            dma((2, nc)),
            dma((2,)),
            dma((2,)),
        ],
        compiler_params=pltpu.CompilerParams(collective_id=0, has_side_effects=True, vmem_limit_bytes=52 * 2**20),
        cost_estimate=pl.CostEstimate(
            flops=8 * rows * ex * half, bytes_accessed=2 * (2 * rows * half + ex * feats) + 4 * rows * ex, transcendentals=0),
    )(query, gram, training)
    return raw * weight[None, :]


def by_gathers(query, gram, training, weight):
    whole_gram = lax.all_gather(gram, "ta", axis=1, tiled=True)
    whole_training = lax.all_gather(training, "pb", axis=1, tiled=True)
    mapped = lax.dot_general(
        whole_gram, whole_training, (((1,), (1,)), ((), ())), preferred_element_type=jnp.float32).astype(jnp.bfloat16)
    whole_query = lax.all_gather(query, "ta", axis=1, tiled=True)
    whole_mapped = lax.all_gather(mapped, "pb", axis=0, tiled=True)
    return jnp.dot(whole_query, whole_mapped, preferred_element_type=jnp.float32) * weight[None, :]


def solution(mesh):
    npb, nta, nrow = mesh.shape["pb"], mesh.shape["ta"], mesh.shape["row"]

    def local(query, gram, training, weight):
        ex, feats = training.shape
        square = query.shape == gram.shape == (feats, npb // 2 * feats)
        fits = (
            nta == 2 and nrow == 2 and npb == 8 and square and ex == 512 and feats % 128 == 0)
        if fits:
            return by_kernel(npb, query, gram, training, weight)
        return by_gathers(query, gram, training, weight)

    placed = (P("pb", "ta"), P("pb", "ta"), P(("row", "ta"), "pb"), P(("row", "ta")))
    return jax.shard_map(
        local, mesh=mesh, in_specs=placed, out_specs=P("pb", ("row", "ta")), check_vma=False
    )
```

```python
import functools

import jax
import jax.numpy as jnp
from jax import lax
from jax.experimental import pallas as pl
from jax.experimental.pallas import tpu as pltpu
from jax.sharding import PartitionSpec as P

MESH = pl.DeviceIdType.MESH
SUB = 2

ORDER = (
    (
        ("over_x", 0, 1), ("over_y", 0, 1), ("own", 0, 0, 1), ("own", 0, 3, 1), ("own", 0, 1, 0), ("own", 0, 2, 1),
        ("over_x", 0, 0), ("pass_on", 0, 0, 1, 1), ("from_y", 0, 1), ("over_y", 0, 0), ("pass_on", 0, 3, 1, 1),
        ("pass_on", 0, 1, 1, 0), ("pass_on", 0, 1, 2, 0), ("over_y", 1, 0), ("own", 0, 3, 0), ("own", 0, 1, 1),
        ("from_x", 0, 0, 0), ("own", 0, 0, 0), ("from_y", 0, 0), ("own", 0, 2, 0), ("over_y", 1, 1),
        ("pass_on", 0, 0, 1, 0), ("pass_on", 0, 0, 2, 1), ("from_x", 0, 1, 1), ("from_x", 0, 0, 1),
        ("pass_on", 0, 0, 2, 0), ("pass_on", 0, 1, 1, 1), ("from_x", 0, 1, 0), ("pass_on", 0, 2, 1, 0),
        ("pass_on", 0, 1, 3, 0), ("over_x", 1, 1), ("sibling", 0), ("pass_on", 0, 1, 2, 1),
        ("pass_on", 0, 0, 3, 0), ("pass_on", 0, 2, 1, 1), ("pass_on", 0, 3, 1, 0), ("from_y", 1, 0),
        ("pass_on", 0, 0, 3, 1),
    ),
    (
        ("pass_on", 0, 1, 3, 1), ("pass_on", 0, 2, 2, 0), ("from_y", 1, 1), ("pass_on", 0, 3, 2, 0),
        ("pass_on", 0, 2, 2, 1),
    ),
    (
        ("pass_on", 0, 3, 2, 1), ("h_sum", 0), ("pass_on", 0, 2, 3, 0), ("own", 1, 0, 0), ("pass_on", 0, 3, 3, 1),
        ("pass_on", 0, 2, 3, 1), ("own", 1, 0, 1),
    ),
    (
        ("pass_on", 1, 0, 1, 0), ("pass_on", 1, 0, 1, 1), ("pass_on", 0, 3, 3, 0), ("from_x", 1, 0, 1),
        ("h_sum", 1), ("own", 1, 1, 0), ("own", 1, 1, 1), ("over_x", 1, 0),
    ),
    (
        ("pass_on", 1, 0, 2, 0), ("pass_on", 1, 1, 1, 1), ("pass_on", 1, 0, 2, 1), ("pass_on", 1, 1, 1, 0),
        ("h_sum", 2), ("from_x", 1, 1, 1), ("own", 1, 2, 1), ("from_x", 1, 1, 0), ("from_x", 1, 0, 0),
        ("pass_on", 1, 1, 2, 0), ("pass_on", 1, 0, 3, 1), ("sibling", 1), ("own", 1, 2, 0), ("h_sum", 3),
        ("pass_on", 1, 2, 1, 1), ("pass_on", 1, 1, 2, 1), ("pass_on", 1, 0, 3, 0),
    ),
    (
        ("pass_on", 1, 1, 3, 0), ("pass_on", 1, 1, 3, 1), ("own", 1, 3, 0), ("pass_on", 1, 2, 1, 0),
    ),
    (
        ("pass_on", 1, 2, 2, 0), ("pass_on", 1, 2, 2, 1), ("own", 1, 3, 1), ("pass_on", 1, 2, 3, 0),
        ("pass_on", 1, 2, 3, 1),
    ),
    (
        ("pass_on", 1, 3, 1, 0), ("pass_on", 1, 3, 1, 1), ("pass_on", 1, 3, 2, 0), ("pass_on", 1, 3, 3, 0),
        ("last_half", 0), ("pass_on", 1, 3, 3, 1), ("pass_on", 1, 3, 2, 1), ("last_half", 1), ("score_sum", 2),
        ("score_sum", 1), ("score_sum", 0), ("score_sum", 3),
    ),
)


def kernel(npb, nc, q_ref, g_ref, t_ref, w_ref, out_ref, q_all, g_all, t_all, h_all, turned, kept, part_out, part_in,
           last_out, last_in, own_sem, z_send, z_recv, y_send, y_recv, x_send, x_recv, s_send, s_recv, p_send, p_recv, l_send, l_recv):
    me = lax.axis_index("pb")
    ta = lax.axis_index("ta")
    row = lax.axis_index("row")
    nz = npb // 2
    z, y = me // 2, me % 2
    up, down, across = {"pb": me + 2}, {"pb": me - 2}, {"pb": z * 2 + 1 - y}
    xp, sib = {"ta": 1 - ta}, {"row": 1 - row}
    rows, half = g_ref.shape
    ex, feats = t_ref.shape
    width = ex // nc
    nh = half // feats // 2
    strip_rows = rows // 2
    has_up, has_down = z < nz - 1, z > 0

    def remote(src, dst, send_sem, recv_sem, device):
        return pltpu.make_async_remote_copy(
            src_ref=src, dst_ref=dst, send_sem=send_sem, recv_sem=recv_sem, device_id=device, device_id_type=MESH)

    def at(start, size):
        return pl.ds(pl.multiple_of(start * size, size), size)

    def own_columns(which, j, which_y, rows_at):
        return (g_ref, q_ref)[which].at[rows_at, at(j * 2 + which_y, feats)]

    def strip(which, which_y, r, block):
        return (g_all, q_all)[which].at[at(which_y * 2 + r, strip_rows), at(block, feats)]

    own_t = pltpu.make_async_copy(t_ref, t_all.at[z], own_sem.at[0])
    own_t.start()
    own = [
        pltpu.make_async_copy(
            own_columns(which, j, y, pl.ds(0, rows)),
            (g_all, q_all)[which].at[at(y, rows), at(ta * nh + j, feats)], own_sem.at[1 + which * nh + j])
        for which in range(2) for j in range(nh)
    ]
    for copy in own:
        copy.start()

    barrier = pltpu.get_barrier_semaphore()

    def greet(device):
        pl.semaphore_signal(barrier, inc=1, device_id=device, device_id_type=MESH)

    for device in (across, xp, sib):
        greet(device)
    pl.when(has_up)(lambda: greet(up))
    pl.when(has_down)(lambda: greet(down))
    pl.semaphore_wait(barrier, 3 + has_up.astype(jnp.int32) + has_down.astype(jnp.int32))

    def place(phase, c, i, block):
        if phase == 0:
            return t_all.at[block, at(c * SUB + i, width // SUB)]
        return h_all.at[c, at(block * SUB + i, rows // SUB)]

    def z_copy(phase, c, i, block, way):
        ref = place(phase, c, i, block)
        return remote(ref, ref, z_send.at[phase, c, i, way, block], z_recv.at[phase, c, i, block], (up, down)[way])

    def send_own(phase, c, i):
        pl.when(has_up)(lambda: z_copy(phase, c, i, z, 0).start())
        pl.when(has_down)(lambda: z_copy(phase, c, i, z, 1).start())

    def pass_on(phase, c, d, i):
        @pl.when(z - d >= 0)
        def _():
            z_copy(phase, c, i, z - d, 0).wait_recv()
            pl.when(has_up)(lambda: z_copy(phase, c, i, z - d, 0).start())

        @pl.when(z + d < nz)
        def _():
            z_copy(phase, c, i, z + d, 1).wait_recv()
            pl.when(has_down)(lambda: z_copy(phase, c, i, z + d, 1).start())

    def finish_sends(phase, c):
        for i in range(SUB):
            for block in range(nz):
                pl.when(has_up & (block <= z))(lambda: z_copy(phase, c, i, block, 0).wait_send())
                pl.when(has_down & (block >= z))(lambda: z_copy(phase, c, i, block, 1).wait_send())

    def y_out(which, j):
        return remote(
            own_columns(which, j, 1 - y, at(row, strip_rows)), strip(which, y, row, ta * nh + j),
            y_send.at[which, j], y_recv.at[which, j], across)

    def y_in(which, j):
        ref = strip(which, 1 - y, row, ta * nh + j)
        return remote(ref, ref, y_send.at[which, j], y_recv.at[which, j], across)

    def x_out(which, kind, j):
        dst = strip(which, (y, 1 - y)[kind], row, ta * nh + j)
        src = own_columns(which, j, y, at(row, strip_rows)) if kind == 0 else dst
        return remote(src, dst, x_send.at[which, kind, j], x_recv.at[which, kind, j], xp)

    def x_in(which, kind, j):
        ref = strip(which, (y, 1 - y)[kind], row, (1 - ta) * nh + j)
        return remote(ref, ref, x_send.at[which, kind, j], x_recv.at[which, kind, j], xp)

    def s_copy(which, kind, j, r):
        ref = strip(which, (y, 1 - y, 1 - y)[kind], r, (ta if kind == 2 else 1 - ta) * nh + j)
        return remote(ref, ref, s_send.at[which, kind, j], s_recv.at[which, kind, j], sib)

    def from_y(which, j):
        y_in(which, j).wait_recv()
        x_out(which, 1, j).start()
        s_copy(which, 2, j, row).start()

    def from_x(which, kind, j):
        x_in(which, kind, j).wait_recv()
        s_copy(which, kind, j, row).start()

    def from_sibling(which):
        for kind in range(3):
            for j in range(nh):
                s_copy(which, kind, j, 1 - row).wait_recv()
        for copy in own[which * nh:(which + 1) * nh]:
            copy.wait()

    def p_copy(phase, c):
        return remote(part_out.at[phase, c], part_in.at[phase, c], p_send.at[phase, c], p_recv.at[phase, c], across)

    tall = rows // 2
    left_lanes = lax.broadcasted_iota(jnp.int32, (tall, width), 1) < width // 2
    last = pl.ds((nc - 1) * width, width)

    def swap_quarters(one, two):
        turn = lambda x: pltpu.roll(x, width // 2, 1)
        return [jnp.where(left_lanes, one, turn(two)), jnp.where(left_lanes, turn(one), two)]

    def last_copy(i):
        return remote(last_out.at[i], last_in.at[i], l_send.at[i], l_recv.at[i], across)

    def last_product(which_y, i):
        sums = []
        for k in range(2):
            sums.append(sum(
                jnp.dot(q_all[at(which_y, rows), block * feats + k * tall:block * feats + (k + 1) * tall],
                        h_all[nc - 1, (block * 2 + i) * tall:(block * 2 + i + 1) * tall, :],
                        preferred_element_type=jnp.float32)
                for block in range(nz)))
        return sums[0] + pltpu.roll(sums[1], width // 2, 1)

    def last_half(i):
        part = last_product(1 - y, i)
        last_out[i] = swap_quarters(part[:tall], part[tall:])[0]
        last_copy(i).start()
        part = last_product(y, i)
        if i == 0:
            out_ref[:, last] = part
        else:
            both = jnp.concatenate([left_lanes, left_lanes], axis=0)
            out_ref[:, last] = jnp.where(both, out_ref[:, last], pltpu.roll(part, width // 2, 1))

    def last_combine():
        for i in range(2):
            last_copy(i).wait_recv()
        upper, lower = swap_quarters(last_in[0], last_in[1])
        weight = w_ref[:, last]
        out_ref[:tall, last] = (out_ref[:tall, last] + upper) * weight
        out_ref[tall:, last] = (out_ref[tall:, last] + lower) * weight

    def h_partial(c):
        for block in range(nz):
            turned[block * feats:(block + 1) * feats, :] = t_all[block, at(c, width), :].T

        def product(which_y):
            return jnp.dot(g_all[at(which_y, rows), :], turned[...], preferred_element_type=jnp.float32)

        part_out[0, c] = product(1 - y)
        p_copy(0, c).start()
        kept[c] = product(y)

    def h_combine(c):
        p_copy(0, c).wait_recv()
        h = kept[c] + part_in[0, c]
        if c == nc - 1:
            h = jnp.concatenate(swap_quarters(h[:tall], h[tall:]), axis=0)
        h_all[c, at(z, rows), :] = h.astype(jnp.bfloat16)

    def score_partial(c):
        def product(which_y):
            return jnp.dot(q_all[at(which_y, rows), :], h_all[c], preferred_element_type=jnp.float32)

        part_out[1, c] = product(1 - y)
        p_copy(1, c).start()
        out_ref[:, at(c, width)] = product(y)

    def score_combine(c):
        if c == nc - 1:
            return last_combine()
        p_copy(1, c).wait_recv()
        span = at(c, width)
        out_ref[:, span] = (out_ref[:, span] + part_in[1, c]) * w_ref[:, span]

    own_t.wait()
    steps = {
        "own": send_own, "pass_on": pass_on, "over_y": lambda which, j: y_out(which, j).start(),
        "over_x": lambda which, j: x_out(which, 0, j).start(), "from_y": from_y, "from_x": from_x,
        "sibling": from_sibling, "h_sum": h_combine, "score_sum": score_combine, "last_half": last_half,
    }

    def stage(s, carry):
        for k, group in enumerate(ORDER):
            @pl.when(s == k)
            def _():
                for name, *which in group:
                    steps[name](*which)

        pl.when(s < nc)(lambda: h_partial(s))
        pl.when((s >= nc) & (s < 2 * nc - 1))(lambda: score_partial(s - nc))
        return carry

    lax.fori_loop(0, 2 * nc, stage, 0)

    def drain(c, carry):
        for phase in range(2):
            finish_sends(phase, c)
        p_copy(0, c).wait_send()
        pl.when(c < nc - 1)(lambda: p_copy(1, c).wait_send())
        return carry

    lax.fori_loop(0, nc, drain, 0)
    for i in range(2):
        last_copy(i).wait_send()
    for which in range(2):
        for j in range(nh):
            y_out(which, j).wait_send()
            for kind in range(2):
                x_out(which, kind, j).wait_send()
            for kind in range(3):
                s_copy(which, kind, j, row).wait_send()


def by_kernel(npb, query, gram, training, weight):
    rows, half = gram.shape
    ex, feats = training.shape
    width = 128
    nc = ex // width
    nz = npb // 2
    nh = half // feats // 2
    anywhere = pl.BlockSpec(memory_space=pl.ANY)
    dma = pltpu.SemaphoreType.DMA
    return pl.pallas_call(
        functools.partial(kernel, npb, nc),
        out_shape=jax.ShapeDtypeStruct((rows, ex), jnp.float32),
        in_specs=[anywhere] * 3 + [pl.BlockSpec(memory_space=pltpu.VMEM)],
        out_specs=pl.BlockSpec(memory_space=pltpu.VMEM),
        scratch_shapes=[
            pltpu.VMEM((2 * rows, half), jnp.bfloat16),
            pltpu.VMEM((2 * rows, half), jnp.bfloat16),
            pltpu.VMEM((nz, ex, feats), jnp.bfloat16),
            pltpu.VMEM((nc, half, width), jnp.bfloat16),
            pltpu.VMEM((half, width), jnp.bfloat16),
            pltpu.VMEM((nc, rows, width), jnp.float32),
            pltpu.VMEM((2, nc, rows, width), jnp.float32),
            pltpu.VMEM((2, nc, rows, width), jnp.float32),
            pltpu.VMEM((2, rows // 2, width), jnp.float32),
            pltpu.VMEM((2, rows // 2, width), jnp.float32),
            dma((1 + 2 * nh,)),
            dma((2, nc, SUB, 2, nz)),
            dma((2, nc, SUB, nz)),
            dma((2, nh)),
            dma((2, nh)),
            dma((2, 2, nh)),
            dma((2, 2, nh)),
            dma((2, 3, nh)),
            dma((2, 3, nh)),
            dma((2, nc)),
            dma((2, nc)),
            dma((2,)),
            dma((2,)),
        ],
        compiler_params=pltpu.CompilerParams(collective_id=0, has_side_effects=True, vmem_limit_bytes=52 * 2**20),
        cost_estimate=pl.CostEstimate(
            flops=8 * rows * ex * half, bytes_accessed=2 * (2 * rows * half + ex * feats) + 4 * rows * ex, transcendentals=0),
    )(query, gram, training, weight[None, :])


def by_gathers(query, gram, training, weight):
    whole_gram = lax.all_gather(gram, "ta", axis=1, tiled=True)
    whole_training = lax.all_gather(training, "pb", axis=1, tiled=True)
    mapped = lax.dot_general(
        whole_gram, whole_training, (((1,), (1,)), ((), ())), preferred_element_type=jnp.float32).astype(jnp.bfloat16)
    whole_query = lax.all_gather(query, "ta", axis=1, tiled=True)
    whole_mapped = lax.all_gather(mapped, "pb", axis=0, tiled=True)
    return jnp.dot(whole_query, whole_mapped, preferred_element_type=jnp.float32) * weight[None, :]


def solution(mesh):
    npb, nta, nrow = mesh.shape["pb"], mesh.shape["ta"], mesh.shape["row"]

    def local(query, gram, training, weight):
        ex, feats = training.shape
        square = query.shape == gram.shape == (feats, npb // 2 * feats)
        fits = (
            nta == 2 and nrow == 2 and npb == 8 and square and ex == 512 and feats % 128 == 0)
        if fits:
            return by_kernel(npb, query, gram, training, weight)
        return by_gathers(query, gram, training, weight)

    placed = (P("pb", "ta"), P("pb", "ta"), P(("row", "ta"), "pb"), P(("row", "ta")))
    return jax.shard_map(
        local, mesh=mesh, in_specs=placed, out_specs=P("pb", ("row", "ta")), check_vma=False
    )
```
